128 devices in a mesh: row: 8 (over y, core), col: 16 (over x, z).
Axes of the slice: x: 4, y: 4, z: 4, core: 2. Of those that a mesh axis runs over, the one named last changes fastest.
Arguments:
- query_embed: bfloat16 [16384, 2048], P('row', 'col'), may hold values from -40 to 40, as said below
- gist_embed: bfloat16 [16384, 2048], P('col', 'row'), may hold values from -40 to 40, as said below
- positive: int32 [16384], P('row'), may hold values from 0 to 16383, each once
Outputs:
- loss_value: float32 [], replicated
- query_grad: float32 [16384, 2048], P('row', 'col')
- gist_grad: float32 [16384, 2048], P('col', 'row')
The draws below stay inside these ranges and needn't reach their ends.
Inputs may be any that keep to these rules, and one draw needn't show every extreme that they name: `positive`: A permutation of the gist summaries. `query_embed`: Real-valued embeddings. `gist_embed`: Real-valued embeddings.
All inputs are finite; a program needn't handle non-finite values.
Results may differ from the reference program's by a relative error of at most 0.0013.
Values may be sent and summed in bfloat16 or wider, within the bound.
A program may use at most 128 MiB of HBM per device.

```python
import math
import jax
import jax.numpy as jnp
from jax import lax

D = 2048
Q_DEV = 2048
QUERIES = 16384


def rising_scale(low, high):
    position = jnp.arange(QUERIES, dtype=jnp.float32) / float(max(QUERIES - 1, 1))
    return (low + (high - low) * position)[:, None]


def draw_query_embed(key, part):
    own_key = jax.random.fold_in(key, 5)
    own = jnp.clip(jax.random.normal(own_key, (QUERIES, D), jnp.float32), -6.0, 6.0)
    return (own * rising_scale(0.6, 1.8)).astype(jnp.bfloat16)


def draw_gist_embed(key, part):
    own_key = jax.random.fold_in(key, 9)
    own = jnp.clip(jax.random.normal(own_key, (QUERIES, D), jnp.float32), -6.0, 6.0)
    return (own * rising_scale(0.6, 1.8)).astype(jnp.bfloat16)


def setup_inputs(seed: int = 0) -> dict:
    arg_keys = jax.random.split(jax.random.key(seed), 4)
    query_embed = draw_query_embed(jax.random.fold_in(arg_keys[3], 71), 0)
    gist_embed = draw_gist_embed(jax.random.fold_in(arg_keys[3], 71), 0)
    positive = jax.random.permutation(arg_keys[2], QUERIES).astype(jnp.int32)
    return dict(query_embed=query_embed, gist_embed=gist_embed, positive=positive)


def reference(query_embed, gist_embed, positive):
    count_all = query_embed.shape[0]
    factor = 1.0 / math.sqrt(D)
    blocks = count_all // Q_DEV
    gist_blocks = gist_embed.reshape(blocks, Q_DEV, D)

    def column_stats(gist_block):
        scores_t = jnp.dot(gist_block, query_embed.T, preferred_element_type=jnp.float32) * factor
        col_peak = lax.optimization_barrier(jnp.max(scores_t, axis=1))
        return col_peak + jnp.log(lax.optimization_barrier(jnp.sum(jnp.exp(scores_t - col_peak[:, None]), axis=1)))
    col_lse = lax.map(column_stats, gist_blocks).reshape(count_all)
    query_blocks = query_embed.reshape(blocks, Q_DEV, D)
    positive_blocks = positive.reshape(blocks, Q_DEV)
    columns = jnp.arange(count_all, dtype=jnp.int32)

    def block_step(state_now, inputs):
        gist_acc, lse_sum, pos_sum = state_now
        query_block, pos_block = inputs
        scores = jnp.dot(query_block, gist_embed.T, preferred_element_type=jnp.float32) * factor
        row_peak = lax.optimization_barrier(jnp.max(scores, axis=1))
        row_lse = row_peak + jnp.log(lax.optimization_barrier(jnp.sum(jnp.exp(scores - row_peak[:, None]), axis=1)))
        onehot = (pos_block[:, None] == columns[None, :]).astype(jnp.float32)
        dlogit = (jnp.exp(scores - row_lse[:, None]) + jnp.exp(scores - col_lse[None, :]) - 2.0 * onehot).astype(jnp.bfloat16)
        query_part = jnp.dot(dlogit, gist_embed, preferred_element_type=jnp.float32)
        gist_acc = gist_acc + lax.dot_general(dlogit, query_block, (((0,), (0,)), ((), ())), preferred_element_type=jnp.float32)
        return ((gist_acc, lse_sum + jnp.sum(row_lse), pos_sum + jnp.sum(scores * onehot)), query_part)
    start_state = (jnp.zeros((count_all, D), jnp.float32), jnp.zeros((), jnp.float32), jnp.zeros((), jnp.float32))
    final_state, query_parts = lax.scan(block_step, start_state, (query_blocks, positive_blocks))
    gist_grad, lse_sum, pos_sum = final_state
    query_grad = query_parts.reshape(count_all, D)
    loss_value = (lse_sum + jnp.sum(col_lse) - 2.0 * pos_sum) / (2.0 * count_all)
    return (loss_value, query_grad, gist_grad)
```

```python
import functools
import math

import jax
import jax.numpy as jnp
from jax import lax
from jax.experimental import pallas as pl
from jax.experimental.pallas import tpu as pltpu
from jax.sharding import PartitionSpec as P

D = 2048
MESH = pl.DeviceIdType.MESH
LOG2E = 1.4426950408889634
LN2 = 0.6931471805599453
F32 = jnp.float32
BF16 = jnp.bfloat16
I16 = jnp.int16
TOP = 32752.0

A, BP, BM, C, DD = 0, 2, 6, 10, 12
R1, R2, R3P, R3M, R4 = 14, 16, 18, 22, 26
NMSG = 28


def where_am_i():
    row = lax.axis_index("row")
    col = lax.axis_index("col")
    return lax.div(col, 4), lax.div(row, 2), lax.rem(col, 4), lax.rem(row, 2)


def mod4(v):
    return lax.rem(v + 8, 4)


def encode(x):
    rows, cols = x.shape
    x3 = x.reshape(rows // 8, 8, cols)
    top = jnp.maximum(jnp.max(jnp.abs(x3), axis=0), 1e-30)
    inv = TOP / top
    code = jnp.round(x3 * inv[None]).reshape(rows, cols).astype(jnp.int32).astype(I16)
    return code, top * (1.0 / TOP)


def decode(code, scale):
    rows, cols = code.shape
    x3 = code.astype(jnp.int32).astype(F32).reshape(rows // 8, 8, cols)
    return (x3 * scale[None]).reshape(rows, cols)


def kernel(
    q_ref, g_ref, pos_ref, loss_ref, qg_ref, gg_ref,
    qbuf, gbuf, s_buf, dl, dlt, posbuf,
    ml, sl, mc, sc, rowst, colst0, colst, rl_t, cl_t, pos_t, pacc,
    qr_s, qr_r, qr_ss, qr_sr, gr_s, gr_r, gr_ss, gr_sr,
    cx_s, cx_r, cx_ss, cx_sr, pg, qout, lossbuf,
    qs, qv, gs, gv, es, ev, ms, mv, rss, rsv, css, csv, ls, lv,
    qss, qsv, gss, gsv, xs, xv, xss, xsv, lsem,
):
    x, y, z, k = where_am_i()
    h = lax.div(x, 2)
    e = lax.rem(x, 2)
    xi = x + 1 - 2 * e
    xo = 3 - x
    xio = 3 - xi
    xj = [x, xo, xi, xio]

    def dev(xx, yy, zz, kk):
        return (yy * 2 + kk, xx * 4 + zz)

    core = dev(x, y, z, 1 - k)
    part_q = dev(xi, y, z, k)
    part_g = dev(xo, y, z, k)
    part_g2 = dev(xo, y, z, 1 - k)
    zpeer = {d: dev(x, y, mod4(z + d), k) for d in (1, 2, 3)}
    ypeer = {d: dev(x, mod4(y + d), z, k) for d in (1, 2, 3)}
    zipeer = {d: dev(xi, y, mod4(z + d), k) for d in (1, 2, 3)}
    yopeer = {d: dev(xo, mod4(y + d), z, k) for d in (1, 2, 3)}
    everyone = [core, part_q, part_g, part_g2]
    for group in (zpeer, ypeer, zipeer, yopeer):
        everyone += list(group.values())

    barrier = pltpu.get_barrier_semaphore()
    for other in everyone:
        pl.semaphore_signal(barrier, inc=1, device_id=other, device_id_type=MESH)

    def rc(src, dst, s, v, to):
        return pltpu.make_async_remote_copy(
            src_ref=src, dst_ref=dst, send_sem=s, recv_sem=v, device_id=to, device_id_type=MESH
        )

    gl = [
        pltpu.make_async_copy(g_ref.at[pl.ds(t * 512, 512)], gbuf.at[y, k, t], lsem.at[t])
        for t in range(2)
    ]
    for c in gl:
        c.start()
    here = pltpu.make_async_copy(q_ref.at[pl.ds(k * 1024, 1024)], qbuf.at[z, 0], lsem.at[2])
    posc = pltpu.make_async_copy(pos_ref, posbuf.at[k], lsem.at[3])
    posc.start()
    pl.semaphore_wait(barrier, len(everyone))

    pos_copy = rc(pos_ref, posbuf.at[k], ms.at[0], mv.at[0], core)
    pos_copy.start()
    q1c = rc(q_ref.at[pl.ds((1 - k) * 1024, 1024)], qbuf.at[z, 0], ms.at[1], mv.at[1], core)
    q1o = [
        rc(q_ref.at[pl.ds(kk * 1024, 1024)], qbuf.at[z, 1], ms.at[2 + kk], mv.at[2],
           dev(xo, y, z, kk))
        for kk in range(2)
    ]

    @pl.when(h == k)
    def _():
        here.start()
        q1c.start()

    @pl.when(h != k)
    def _():
        q1o[0].start()
        q1o[1].start()

    def qp(i, t):
        return qbuf.at[i, t]

    def gp(i, t):
        return gbuf.at[i, k, t]

    def ring(buf, r, sems, semv, plus, minus, partner):
        def msg(src_i, src_t, dst_t, idx, to):
            return rc(buf(src_i, src_t), buf(src_i, dst_t), sems.at[idx], semv.at[idx], to)

        before, after, far = mod4(r - 1), mod4(r + 1), mod4(r + 2)
        m = {}
        for t in range(2):
            m["a", t] = msg(r, t, t + 2, A + t, partner)
            m["d", t] = msg(far, t, t + 2, DD + t, partner)
        for t in range(4):
            m["p", t] = msg(r, t, t, BP + t, plus)
            m["m", t] = msg(r, t, t, BM + t, minus)
        m["c", 0] = msg(before, 0, 0, C, plus)
        m["c", 1] = msg(after, 1, 1, C + 1, minus)
        return m

    qm = ring(qp, z, qs, qv, zpeer[1], zpeer[3], part_q)
    gm = ring(gp, y, gs, gv, ypeer[1], ypeer[3], part_g)

    for c in gl:
        c.wait()
    for t in range(2):
        gm["p", t].start()
        gm["m", t].start()
        gm["a", t].start()

    def to_core(idx, i, t):
        return rc(gp(i, t), gp(i, t), es.at[idx, t], ev.at[idx, t], core)

    ecopies = []

    def start_core(idx, i, t):
        c = to_core(idx, i, t)
        c.start()
        ecopies.append(c)

    start_core(0, y, 0)
    start_core(0, y, 1)

    @pl.when(h == k)
    def _():
        here.wait()

    @pl.when(h != k)
    def _():
        q1c.wait_recv()

    for d in ("p", "m", "a"):
        qm[d, 0].start()
    q1o[0].wait_recv()
    for d in ("p", "m", "a"):
        qm[d, 1].start()

    yb, ya, yf = mod4(y - 1), mod4(y + 1), mod4(y + 2)
    qm["p", 0].wait_recv()
    qm["c", 0].start()
    gm["p", 0].wait_recv()
    gm["c", 0].start()
    start_core(3, yb, 0)
    gm["m", 0].wait_recv()
    start_core(1, ya, 0)
    qm["m", 1].wait_recv()
    qm["c", 1].start()
    gm["m", 1].wait_recv()
    gm["c", 1].start()
    start_core(1, ya, 1)
    gm["p", 1].wait_recv()
    start_core(3, yb, 1)
    for t in range(2):
        qm["a", t].wait_recv()
        qm["p", t + 2].start()
        qm["m", t + 2].start()
        gm["a", t].wait_recv()
        gm["p", t + 2].start()
        gm["m", t + 2].start()
        start_core(0, y, t + 2)
    for t in range(2):
        qm["c", t].wait_recv()
        qm["d", t].start()
        gm["c", t].wait_recv()
        gm["d", t].start()
        start_core(2, yf, t)
    for t in range(2, 4):
        gm["p", t].wait_recv()
        start_core(3, yb, t)
        gm["m", t].wait_recv()
        start_core(1, ya, t)
        qm["p", t].wait_recv()
        qm["m", t].wait_recv()
    qm["m", 0].wait_recv()
    qm["p", 1].wait_recv()
    for t in range(2):
        gm["d", t].wait_recv()
        start_core(2, yf, t + 2)
        qm["d", t].wait_recv()
    for c in ecopies:
        c.wait_recv()
    posc.wait()
    pos_copy.wait_recv()

    scale = LOG2E / math.sqrt(D)

    def logits(t, carry):
        g = jnp.concatenate([gbuf[xj[j], m, t] for j in range(4) for m in range(2)], axis=1)

        def rows_of(b, carry):
            r = pl.ds(pl.multiple_of(b * 256, 256), 256)
            q = jnp.concatenate(
                [qbuf[2 * m + u, j, r, :] for j in range(4) for m in range(2) for u in range(2)],
                axis=1,
            )
            s = lax.dot_general(q, g, (((1,), (1,)), ((), ())), preferred_element_type=F32)
            s = s * scale
            for u in range(4):
                s_buf[t * 4 + u, r, :] = s[:, u * 128:(u + 1) * 128]
            return carry

        return lax.fori_loop(0, 4, rows_of, carry)

    lax.fori_loop(0, 4, logits, 0)

    mc[...] = jnp.full_like(mc, -jnp.inf)
    sc[...] = jnp.zeros_like(sc)

    def stats(a, carry):
        r = pl.ds(pl.multiple_of(a * 128, 128), 128)
        top = s_buf[0, r, :]
        for c in range(1, 16):
            top = jnp.maximum(top, s_buf[c, r, :])
        total = jnp.zeros_like(top)
        for c in range(16):
            v = s_buf[c, r, :]
            total = total + jnp.exp2(v - top)
            v3 = v.reshape(16, 8, 128)
            old = mc[c]
            new = jnp.maximum(old, jnp.max(v3, axis=0))
            mc[c] = new
            sc[c] = sc[c] * jnp.exp2(old - new) + jnp.sum(jnp.exp2(v3 - new[None]), axis=0)
        tt = top.T
        peak = jnp.max(tt, axis=0, keepdims=True)
        one = jnp.sum(total.T * jnp.exp2(tt - peak), axis=0, keepdims=True)
        ml[pl.ds(a, 1), :] = peak
        sl[pl.ds(a, 1), :] = one
        return carry

    lax.fori_loop(0, 8, stats, 0)

    for c in range(16):
        peak = jnp.max(mc[c], axis=0, keepdims=True)
        one = jnp.sum(sc[c] * jnp.exp2(mc[c] - peak), axis=0, keepdims=True)
        colst0[0, c // 8, 0, pl.ds(c % 8, 1), :] = peak
        colst0[0, c // 8, 1, pl.ds(c % 8, 1), :] = one
    ccopy = rc(colst0.at[0], colst0.at[1], ms.at[4], mv.at[4], core)
    ccopy.start()

    me_row = e * 4 + z
    rowst[me_row, 0] = ml[...]
    rowst[me_row, 1] = sl[...]
    rcopies = []
    for d in (1, 2, 3):
        for n, to in ((d - 1, zpeer[d]), (d + 2, zipeer[d])):
            rcopies.append(rc(rowst.at[me_row], rowst.at[me_row], rss.at[n], rsv.at[n], to))
    rcopies.append(rc(rowst.at[me_row], rowst.at[me_row], rss.at[6], rsv.at[6], part_q))
    for c in rcopies:
        c.start()

    ccopy.wait()
    for i in range(2):
        m0, m1 = colst0[0, i, 0], colst0[1, i, 0]
        peak = jnp.maximum(m0, m1)
        colst[0, y, i, 0] = peak
        colst[0, y, i, 1] = colst0[0, i, 1] * jnp.exp2(m0 - peak) + colst0[1, i, 1] * jnp.exp2(
            m1 - peak
        )
    kcopies = []
    for d in (1, 2, 3):
        kcopies.append(rc(colst.at[0, y], colst.at[0, y], css.at[d - 1], csv.at[d - 1], ypeer[d]))
        kcopies.append(rc(colst.at[0, y], colst.at[1, y], css.at[d + 2], csv.at[d + 2], yopeer[d]))
    kcopies.append(rc(colst.at[0, y], colst.at[1, y], css.at[6], csv.at[6], part_g))
    for c in kcopies:
        c.start()

    def pos_cols(a, carry):
        r = pl.ds(pl.multiple_of(a * 128, 128), 128)
        v = posbuf[h, pl.ds(k * 8 + a, 1), :]
        pos_t[r, :] = jnp.broadcast_to(v, (128, 128)).T
        return carry

    lax.fori_loop(0, 8, pos_cols, 0)

    for c in rcopies:
        c.wait()
    peak = rowst[0, 0]
    for n in range(1, 8):
        peak = jnp.maximum(peak, rowst[n, 0])
    tot = jnp.zeros_like(peak)
    for n in range(8):
        tot = tot + rowst[n, 1] * jnp.exp2(rowst[n, 0] - peak)
    row_lse = peak + jnp.log2(tot)
    ml[...] = row_lse

    def row_cols(a, carry):
        r = pl.ds(pl.multiple_of(a * 128, 128), 128)
        rl_t[r, :] = jnp.broadcast_to(ml[pl.ds(a, 1), :], (128, 128)).T
        return carry

    lax.fori_loop(0, 8, row_cols, 0)

    for c in kcopies:
        c.wait()
    for i in range(2):
        peak = colst[0, 0, i, 0]
        for n in range(4):
            peak = jnp.maximum(jnp.maximum(peak, colst[0, n, i, 0]), colst[1, n, 1 - i, 0])
        tot = jnp.zeros_like(peak)
        for n in range(4):
            a0 = colst[0, n, i, 1] * jnp.exp2(colst[0, n, i, 0] - peak)
            a1 = colst[1, n, 1 - i, 1] * jnp.exp2(colst[1, n, 1 - i, 0] - peak)
            tot = tot + (a0 + a1)
        cl_t[pl.ds(i * 8, 8), :] = peak + jnp.log2(tot)

    pacc[...] = jnp.zeros_like(pacc)
    start0 = (x * 4 + z) * 1024
    start1 = (xo * 4 + z) * 1024

    def dlogit(a, carry):
        r = pl.ds(pl.multiple_of(a * 128, 128), 128)
        rl = rl_t[r, :]
        pos = pos_t[r, :]
        lane = lax.broadcasted_iota(jnp.int32, (128, 128), 1)
        acc = jnp.zeros((8, 128), F32)
        for c in range(16):
            base = (start0 if c < 8 else start1) + (c % 8) * 128
            off = pos - base
            v = s_buf[c, r, :]
            hot = off == lane
            p = jnp.exp2(v - rl) + jnp.exp2(v - cl_t[pl.ds(c, 1), :])
            p = jnp.where(hot, p - 2.0, p)
            acc = acc + jnp.sum(jnp.where(hot, v, 0.0).reshape(16, 8, 128), axis=0)
            p = p.astype(BF16)
            dl[r, c * 128:(c + 1) * 128] = p
            dlt[c * 128:(c + 1) * 128, r] = p.T
        pacc[...] += acc
        return carry

    lax.fori_loop(0, 8, dlogit, 0)

    sub = lax.broadcasted_iota(jnp.int32, (8, 128), 0)
    part = jnp.where(sub == me_row, row_lse, 0.0) + jnp.where(sub == y * 2 + k, cl_t[0:8, :], 0.0)
    loss_part = (part - 2.0 * pacc[...]) * LN2
    lcount = [0]

    def loss_pair(v, to):
        n = lcount[0]
        lcount[0] += 1
        lossbuf[2 * n] = v
        c = rc(lossbuf.at[2 * n], lossbuf.at[2 * n + 1], ls.at[n], lv.at[n], to)
        c.start()
        c.wait()
        return v + lossbuf[2 * n + 1]

    def loss_four(v, r, peers, base, sem):
        lossbuf[base + r] = v
        cs = [
            rc(lossbuf.at[base + r], lossbuf.at[base + r], ls.at[sem + d], lv.at[sem + d], peers[d])
            for d in (1, 2, 3)
        ]
        for c in cs:
            c.start()
        for c in cs:
            c.wait()
        return (lossbuf[base] + lossbuf[base + 1]) + (lossbuf[base + 2] + lossbuf[base + 3])

    def grad_q(t):
        for m in range(2):
            g = jnp.concatenate([gbuf[xj[t], m, i] for i in range(4)], axis=0)

            def body(b, carry):
                r = pl.ds(pl.multiple_of(b * 256, 256), 256)
                o = jnp.dot(dl[r, :], g, preferred_element_type=F32)
                s_buf[2 * m * 4 + t, r, :] = o[:, :128]
                s_buf[(2 * m + 1) * 4 + t, r, :] = o[:, 128:]
                return carry

            lax.fori_loop(0, 4, body, 0)

    def grad_g(t, i, kk):
        j = jnp.where(i == x, 0, jnp.where(i == xo, 1, jnp.where(i == xi, 2, 3)))
        q = jnp.concatenate([qbuf[2 * kk, j], qbuf[2 * kk + 1, j]], axis=1)
        return jnp.dot(dlt[t * 512:(t + 1) * 512, :], q, preferred_element_type=F32)

    sent = []

    def send(v, bufs, n, sems, semv, ssems, ssemv, idx, to):
        s, r, ss, sr = bufs
        code, sca = encode(v)
        s[n] = code
        ss[n] = sca
        c1 = rc(s.at[n], r.at[n], sems.at[idx], semv.at[idx], to)
        c2 = rc(ss.at[n], sr.at[n], ssems.at[n], ssemv.at[n], to)
        c1.start()
        c2.start()
        sent.extend((c1, c2))
        return c1, c2

    def take(c, bufs, n):
        c[0].wait_recv()
        c[1].wait_recv()
        return decode(bufs[1][n], bufs[3][n])

    qb = (qr_s, qr_r, qr_ss, qr_sr)
    gb = (gr_s, gr_r, gr_ss, gr_sr)
    B0 = R1

    def sender(bufs, sems, semv, ssems, ssemv):
        return lambda v, idx, to: send(v, bufs, idx - B0, sems, semv, ssems, ssemv, idx, to)

    send_q = sender(qb, qs, qv, qss, qsv)
    send_g = sender(gb, gs, gv, gss, gsv)

    def pq(rel, t):
        return s_buf[mod4(z + rel) * 4 + t]

    def grad_g_foreign(t):
        for rel in range(4):
            code, sca = encode(grad_g(t, mod4(y + rel), 1 - k))
            cx_s[t % 2, rel] = code
            cx_ss[t % 2, rel] = sca
        c1 = rc(cx_s.at[t % 2], cx_r.at[t], xs.at[t], xv.at[t], core)
        c2 = rc(cx_ss.at[t % 2], cx_sr.at[t], xss.at[t], xsv.at[t], core)
        c1.start()
        c2.start()
        return c1, c2

    def reduce_piece(t, get, sendf, plus, minus, partner, msgs, bufs, hold):
        if t >= 2:
            msgs["1", t] = sendf(get(2), R1 + t - 2, partner)
        if t != 0:
            msgs["p", t] = sendf(get(1), R3P + t, plus)
        if t != 1:
            msgs["m", t] = sendf(get(3), R3M + t, minus)
        if t < 2:
            v = get(2) + take(msgs["1", t + 2], bufs, R1 + t - B0)
            msgs["2", t] = sendf(v, R2 + t, plus if t == 0 else minus)

    qmsg, gmsg = {}, {}
    xmsg = {}
    gcache = {}
    for t in (2, 3, 1, 0):
        if t in (1, 0):
            for c in xmsg[t + 2]:
                c.wait_send()
        xmsg[t] = grad_g_foreign(t)
        grad_q(t)
        reduce_piece(t, lambda rel: pq(rel, t), send_q, zpeer[1], zpeer[3], part_q, qmsg, qb, None)
        for c in xmsg[t]:
            c.wait_recv()
        for rel in range(4):
            pg[rel, t] = grad_g(t, mod4(y + rel), k) + decode(cx_r[t, rel], cx_sr[t, rel])
        reduce_piece(t, lambda rel: pg[rel, t], send_g, ypeer[1], ypeer[3], part_g, gmsg, gb, None)
    for t in (1, 0):
        for c in xmsg[t]:
            c.wait_send()

    for msgs, bufs, get, sendf, plus, minus in (
        (qmsg, qb, lambda rel, t: pq(rel, t), send_q, zpeer[1], zpeer[3]),
        (gmsg, gb, lambda rel, t: pg[rel, t], send_g, ypeer[1], ypeer[3]),
    ):
        msgs["m", 1] = sendf(get(3, 1) + take(msgs["2", 1], bufs, R2 + 1 - B0), R3M + 1, minus)
        msgs["p", 0] = sendf(get(1, 0) + take(msgs["2", 0], bufs, R2 - B0), R3P, plus)

    loss = loss_pair(loss_part, core)
    loss = loss_pair(loss, part_q)
    loss = loss_pair(loss, part_g)
    loss = loss_four(loss, z, zpeer, 6, 2)
    loss = loss_four(loss, y, ypeer, 10, 5)
    loss = jnp.sum(jnp.sum(loss, axis=0, keepdims=True), axis=1, keepdims=True)
    loss_ref[...] = jnp.broadcast_to(loss * (1.0 / 32768.0), (8, 128))

    def ring_sum(get, msgs, bufs, t):
        v = get(0, t) + take(msgs["p", t], bufs, R3P + t - B0)
        return v + take(msgs["m", t], bufs, R3M + t - B0)

    for t in (2, 3):
        v = ring_sum(lambda rel, t: pq(rel, t), qmsg, qb, t)
        qmsg["4", t] = send_q(v, R4 + t - 2, part_q)
        v = ring_sum(lambda rel, t: pg[rel, t], gmsg, gb, t)
        gmsg["4", t] = send_g(v, R4 + t - 2, part_g)

    def final(get, msgs, bufs, t):
        v = ring_sum(get, msgs, bufs, t)
        return v + take(msgs["4", t + 2], bufs, R4 + t - B0)

    rows_k = pl.ds(k * 1024, 1024)
    qout[1] = final(lambda rel, t: pq(rel, t), qmsg, qb, 1)
    out_far = rc(qout.at[1], qg_ref.at[rows_k], ms.at[5], mv.at[5 + k], dev(xo, y, z, h))
    out_far.start()
    gg_ref[pl.ds(512, 512), :] = final(lambda rel, t: pg[rel, t], gmsg, gb, 1)
    qout[0] = final(lambda rel, t: pq(rel, t), qmsg, qb, 0)
    out_core = rc(qout.at[0], qg_ref.at[rows_k], ms.at[6], mv.at[5 + k], core)
    out_here = pltpu.make_async_copy(qout.at[0], qg_ref.at[rows_k], lsem.at[4])

    @pl.when(h == k)
    def _():
        out_here.start()

    @pl.when(h != k)
    def _():
        out_core.start()

    gg_ref[pl.ds(0, 512), :] = final(lambda rel, t: pg[rel, t], gmsg, gb, 0)

    def got(kk):
        rc(qout.at[0], qg_ref.at[pl.ds(kk * 1024, 1024)], ms.at[6], mv.at[5 + kk], core).wait_recv()

    @pl.when(h == k)
    def _():
        out_here.wait()
        got(1 - k)
        q1c.wait_send()

    @pl.when(h != k)
    def _():
        out_core.wait_send()
        got(0)
        got(1)
        q1o[0].wait_send()
        q1o[1].wait_send()

    out_far.wait_send()
    pos_copy.wait_send()
    for m in (qm, gm):
        for c in m.values():
            c.wait_send()
    for c in ecopies + sent:
        c.wait_send()


def on_device(query_embed, gist_embed, positive):
    pos = positive.reshape(16, 128)
    vm, dma = pltpu.VMEM, pltpu.SemaphoreType.DMA
    nr = NMSG - R1
    scratch = [
        vm((4, 4, 1024, 128), BF16),
        vm((4, 2, 4, 512, 256), BF16),
        vm((16, 1024, 128), F32),
        vm((1024, 2048), BF16),
        vm((2048, 1024), BF16),
        vm((2, 16, 128), jnp.int32),
        vm((8, 128), F32),
        vm((8, 128), F32),
        vm((16, 8, 128), F32),
        vm((16, 8, 128), F32),
        vm((8, 2, 8, 128), F32),
        vm((2, 2, 2, 8, 128), F32),
        vm((2, 4, 2, 2, 8, 128), F32),
        vm((1024, 128), F32),
        vm((16, 128), F32),
        vm((1024, 128), jnp.int32),
        vm((8, 128), F32),
        vm((nr, 1024, 128), I16),
        vm((nr, 1024, 128), I16),
        vm((nr, 8, 128), F32),
        vm((nr, 8, 128), F32),
        vm((nr, 512, 256), I16),
        vm((nr, 512, 256), I16),
        vm((nr, 8, 256), F32),
        vm((nr, 8, 256), F32),
        vm((2, 4, 512, 256), I16),
        vm((4, 4, 512, 256), I16),
        vm((2, 4, 8, 256), F32),
        vm((4, 4, 8, 256), F32),
        vm((4, 4, 512, 256), F32),
        vm((2, 1024, 128), F32),
        vm((14, 8, 128), F32),
        dma((NMSG,)), dma((NMSG,)),
        dma((NMSG,)), dma((NMSG,)),
        dma((4, 4)), dma((4, 4)),
        dma((8,)), dma((8,)),
        dma((7,)), dma((7,)),
        dma((7,)), dma((7,)),
        dma((9,)), dma((9,)),
        dma((nr,)), dma((nr,)),
        dma((nr,)), dma((nr,)),
        dma((4,)), dma((4,)),
        dma((4,)), dma((4,)),
        dma((5,)),
    ]
    loss, qg, gg = pl.pallas_call(
        kernel,
        out_shape=[
            jax.ShapeDtypeStruct((8, 128), F32),
            jax.ShapeDtypeStruct((2048, 128), F32),
            jax.ShapeDtypeStruct((1024, 256), F32),
        ],
        in_specs=[
            pl.BlockSpec(memory_space=pl.ANY),
            pl.BlockSpec(memory_space=pl.ANY),
            pl.BlockSpec(memory_space=pltpu.VMEM),
        ],
        out_specs=[
            pl.BlockSpec(memory_space=pltpu.VMEM),
            pl.BlockSpec(memory_space=pl.ANY),
            pl.BlockSpec(memory_space=pltpu.VMEM),
        ],
        scratch_shapes=scratch,
        compiler_params=pltpu.CompilerParams(
            collective_id=0, has_side_effects=True, vmem_limit_bytes=63 * 2**20
        ),
    )(query_embed, gist_embed, pos)
    return loss[0, 0], qg, gg


def solution(mesh):
    in_specs = (P("row", "col"), P("col", "row"), P("row"))
    out_specs = (P(), P("row", "col"), P("col", "row"))
    return jax.shard_map(
        on_device, mesh=mesh, in_specs=in_specs, out_specs=out_specs, check_vma=False
    )
```

```python
import functools
import math

import jax
import jax.numpy as jnp
from jax import lax
from jax.experimental import pallas as pl
from jax.experimental.pallas import tpu as pltpu
from jax.sharding import PartitionSpec as P

D = 2048
MESH = pl.DeviceIdType.MESH
LOG2E = 1.4426950408889634
LN2 = 0.6931471805599453
F32 = jnp.float32
BF16 = jnp.bfloat16
I16 = jnp.int16
TOP = 32752.0

A, BP, BM, C, DD, NGATHER = 0, 4, 12, 20, 24, 28
R1, R3P, R3M, R2, R3PH, R3MH, R4, NSLOT = 0, 4, 8, 12, 16, 20, 24, 28
OUT = R4


def where_am_i():
    row = lax.axis_index("row")
    col = lax.axis_index("col")
    return lax.div(col, 4), lax.div(row, 2), lax.rem(col, 4), lax.rem(row, 2)


def mod4(v):
    return lax.rem(v + 8, 4)


def encode(x):
    rows, cols = x.shape
    x3 = x.reshape(rows // 8, 8, cols)
    top = jnp.maximum(jnp.max(jnp.abs(x3), axis=0), 1e-30)
    inv = TOP / top
    code = jnp.round(x3 * inv[None]).reshape(rows, cols).astype(jnp.int32).astype(I16)
    return code, top * (1.0 / TOP)


def decode(code, scale):
    rows, cols = code.shape
    x3 = code.astype(jnp.int32).astype(F32).reshape(rows // 8, 8, cols)
    return (x3 * scale[None]).reshape(rows, cols)


def kernel(
    q_ref, g_ref, pos_ref, loss_ref, qg_ref, gg_ref,
    qbuf, gbuf, s_buf, dl, dlt, posbuf,
    ml, sl, mc, sc, rowst, colst0, colst, cl_t, pacc,
    qr_s, qr_r, qr_ss, qr_sr, gr_s, gr_r, gr_ss, gr_sr,
    cx_s, cx_r, cx_ss, cx_sr, pg, qout, gout, qo_r, qo_sr, lossbuf,
    qs, qv, gs, gv, es, ev, ms, mv, rss, rsv, css, csv, ls, lv,
    qcs, qcv, qss, qsv, gcs, gcv, gss, gsv, xs, xv, xss, xsv, ov, ovs, lsem, osem,
):
    x, y, z, k = where_am_i()
    h = lax.div(x, 2)
    e = lax.rem(x, 2)
    xi = x + 1 - 2 * e
    xo = 3 - x
    xio = 3 - xi
    xj = [x, xo, xi, xio]

    def dev(xx, yy, zz, kk):
        return (yy * 2 + kk, xx * 4 + zz)

    core = dev(x, y, z, 1 - k)
    part_q = dev(xi, y, z, k)
    part_g = dev(xo, y, z, k)
    part_g2 = dev(xo, y, z, 1 - k)
    zpeer = {d: dev(x, y, mod4(z + d), k) for d in (1, 2, 3)}
    ypeer = {d: dev(x, mod4(y + d), z, k) for d in (1, 2, 3)}
    zipeer = {d: dev(xi, y, mod4(z + d), k) for d in (1, 2, 3)}
    yopeer = {d: dev(xo, mod4(y + d), z, k) for d in (1, 2, 3)}
    everyone = [core, part_q, part_g, part_g2]
    for group in (zpeer, ypeer, zipeer, yopeer):
        everyone += list(group.values())

    barrier = pltpu.get_barrier_semaphore()
    for other in everyone:
        pl.semaphore_signal(barrier, inc=1, device_id=other, device_id_type=MESH)

    def rc(src, dst, s, v, to):
        return pltpu.make_async_remote_copy(
            src_ref=src, dst_ref=dst, send_sem=s, recv_sem=v, device_id=to, device_id_type=MESH
        )

    gl = [
        pltpu.make_async_copy(g_ref.at[pl.ds(t * 512, 512)], gbuf.at[y, k, t], lsem.at[t])
        for t in range(2)
    ]
    for c in gl:
        c.start()
    here = pltpu.make_async_copy(q_ref.at[pl.ds(k * 1024, 1024)], qbuf.at[z, 0], lsem.at[2])
    posc = pltpu.make_async_copy(pos_ref, posbuf.at[k], lsem.at[3])
    posc.start()
    pl.semaphore_wait(barrier, len(everyone))

    pos_copy = rc(pos_ref, posbuf.at[k], ms.at[0], mv.at[0], core)
    pos_copy.start()
    q1c = rc(q_ref.at[pl.ds((1 - k) * 1024, 1024)], qbuf.at[z, 0], ms.at[1], mv.at[1], core)
    q1o = [
        rc(q_ref.at[pl.ds(kk * 1024 + u * 512, 512)], qbuf.at[z, 1, pl.ds(u * 512, 512)],
           ms.at[2 + kk * 2 + u], mv.at[2 + u], dev(xo, y, z, kk))
        for u in range(2) for kk in range(2)
    ]

    @pl.when(h == k)
    def _():
        here.start()
        q1c.start()

    @pl.when(h != k)
    def _():
        for c in q1o:
            c.start()

    def qp(i, t, u):
        return qbuf.at[i, t, pl.ds(u * 512, 512)]

    def gp(i, t, u):
        return gbuf.at[i, k, t, pl.ds(u * 256, 256)]

    def ring(buf, r, sems, semv, plus, minus, partner):
        def msg(i, t, u, t2, idx, to):
            return rc(buf(i, t, u), buf(i, t2, u), sems.at[idx], semv.at[idx], to)

        before, after, far = mod4(r - 1), mod4(r + 1), mod4(r + 2)
        m = {}
        for t in range(4):
            for u in range(2):
                n = t * 2 + u
                if t < 2:
                    m["a", t, u] = msg(r, t, u, t + 2, A + n, partner)
                    m["d", t, u] = msg(far, t, u, t + 2, DD + n, partner)
                    m["c", t, u] = msg(before if u == 0 else after, t, u, t, C + n,
                                       plus if u == 0 else minus)
                m["p", t, u] = msg(r, t, u, t, BP + n, plus)
                m["m", t, u] = msg(r, t, u, t, BM + n, minus)
        return m

    qm = ring(qp, z, qs, qv, zpeer[1], zpeer[3], part_q)
    gm = ring(gp, y, gs, gv, ypeer[1], ypeer[3], part_g)
    yb, ya, yf = mod4(y - 1), mod4(y + 1), mod4(y + 2)
    ecopies = []

    def start_core(idx, i, t, u):
        c = rc(gp(i, t, u), gp(i, t, u), es.at[idx, t, u], ev.at[idx, t, u], core)
        c.start()
        ecopies.append(c)

    def both(m, t, first):
        u = first
        m["p", t, u].start()
        m["m", t, 1 - u].start()

    def on(m, t):
        m["p", t, 0].wait_recv()
        m["c", t, 0].start()
        m["m", t, 1].wait_recv()
        m["c", t, 1].start()

    for c in gl:
        c.wait()
    both(gm, 0, 0)
    both(gm, 0, 1)
    for t in range(2):
        for u in range(2):
            gm["a", t, u].start()
    both(gm, 1, 0)

    @pl.when(h == k)
    def _():
        here.wait()

    @pl.when(h != k)
    def _():
        q1c.wait_recv()

    both(qm, 0, 0)
    both(qm, 0, 1)
    for u in range(2):
        qm["a", 0, u].start()
    for t in range(2):
        for u in range(2):
            start_core(0, y, t, u)
    on(gm, 0)
    on(qm, 0)
    both(gm, 1, 1)
    q1o[0].wait_recv()
    q1o[2].wait_recv()
    both(qm, 1, 0)
    qm["a", 1, 0].start()
    both(qm, 1, 1)
    qm["a", 1, 1].start()
    start_core(3, yb, 0, 0)
    start_core(1, ya, 0, 1)
    gm["p", 0, 1].wait_recv()
    start_core(3, yb, 0, 1)
    gm["m", 0, 0].wait_recv()
    start_core(1, ya, 0, 0)
    on(gm, 1)
    start_core(3, yb, 1, 0)
    start_core(1, ya, 1, 1)
    for u in range(2):
        gm["c", 0, u].wait_recv()
        gm["d", 0, u].start()
        start_core(2, yf, 0, u)
        qm["c", 0, u].wait_recv()
        qm["d", 0, u].start()
    on(qm, 1)
    for u in range(2):
        gm["a", 0, u].wait_recv()
        gm["p", 2, u].start()
        gm["m", 2, u].start()
        start_core(0, y, 2, u)
        qm["a", 0, u].wait_recv()
        qm["p", 2, u].start()
        qm["m", 2, u].start()
    gm["p", 1, 1].wait_recv()
    start_core(3, yb, 1, 1)
    gm["m", 1, 0].wait_recv()
    start_core(1, ya, 1, 0)
    for u in range(2):
        qm["a", 1, u].wait_recv()
        qm["p", 3, u].start()
        qm["m", 3, u].start()
        gm["a", 1, u].wait_recv()
        gm["p", 3, u].start()
        gm["m", 3, u].start()
        start_core(0, y, 3, u)
    for u in range(2):
        gm["c", 1, u].wait_recv()
        gm["d", 1, u].start()
        start_core(2, yf, 1, u)
        qm["c", 1, u].wait_recv()
        qm["d", 1, u].start()
    for t in range(2, 4):
        for u in range(2):
            gm["p", t, u].wait_recv()
            start_core(3, yb, t, u)
            gm["m", t, u].wait_recv()
            start_core(1, ya, t, u)
            gm["d", t - 2, u].wait_recv()
            start_core(2, yf, t, u)
    for t in range(4):
        for u in range(2):
            if t >= 2 or u == 1:
                qm["p", t, u].wait_recv()
            if t >= 2 or u == 0:
                qm["m", t, u].wait_recv()
            if t < 2:
                qm["d", t, u].wait_recv()
    for c in ecopies:
        c.wait_recv()
    posc.wait()
    pos_copy.wait_recv()

    scale = LOG2E / math.sqrt(D)

    def logits(t, carry):
        g = jnp.concatenate([gbuf[xj[j], m, t] for j in range(4) for m in range(2)], axis=1)

        q = jnp.concatenate(
            [qbuf[2 * m + u, j] for j in range(4) for m in range(2) for u in range(2)], axis=1
        )
        s = lax.dot_general(q, g, (((1,), (1,)), ((), ())), preferred_element_type=F32)
        s = s * scale
        for u in range(4):
            s_buf[t * 4 + u] = s[:, u * 128:(u + 1) * 128]
        return carry

    lax.fori_loop(0, 4, logits, 0)

    mc[...] = jnp.full_like(mc, -jnp.inf)
    sc[...] = jnp.zeros_like(sc)

    def stats(a, carry):
        r = pl.ds(pl.multiple_of(a * 128, 128), 128)
        top = s_buf[0, r, :]
        for c in range(1, 16):
            top = jnp.maximum(top, s_buf[c, r, :])
        total = jnp.zeros_like(top)
        for c in range(16):
            v = s_buf[c, r, :]
            total = total + jnp.exp2(v - top)
            v3 = v.reshape(16, 8, 128)
            old = mc[c]
            new = jnp.maximum(old, jnp.max(v3, axis=0))
            mc[c] = new
            sc[c] = sc[c] * jnp.exp2(old - new) + jnp.sum(jnp.exp2(v3 - new[None]), axis=0)
        tt = top.T
        peak = jnp.max(tt, axis=0, keepdims=True)
        one = jnp.sum(total.T * jnp.exp2(tt - peak), axis=0, keepdims=True)
        ml[pl.ds(a, 1), :] = peak
        sl[pl.ds(a, 1), :] = one
        return carry

    lax.fori_loop(0, 8, stats, 0)

    for c in range(16):
        peak = jnp.max(mc[c], axis=0, keepdims=True)
        one = jnp.sum(sc[c] * jnp.exp2(mc[c] - peak), axis=0, keepdims=True)
        colst0[0, c // 8, 0, pl.ds(c % 8, 1), :] = peak
        colst0[0, c // 8, 1, pl.ds(c % 8, 1), :] = one
    ccopy = rc(colst0.at[0], colst0.at[1], ms.at[6], mv.at[4], core)
    ccopy.start()

    me_row = e * 4 + z
    rowst[me_row, 0] = ml[...]
    rowst[me_row, 1] = sl[...]
    rcopies = []
    for d in (1, 2, 3):
        for n, to in ((d - 1, zpeer[d]), (d + 2, zipeer[d])):
            rcopies.append(rc(rowst.at[me_row], rowst.at[me_row], rss.at[n], rsv.at[n], to))
    rcopies.append(rc(rowst.at[me_row], rowst.at[me_row], rss.at[6], rsv.at[6], part_q))
    for c in rcopies:
        c.start()

    ccopy.wait()
    for i in range(2):
        m0, m1 = colst0[0, i, 0], colst0[1, i, 0]
        peak = jnp.maximum(m0, m1)
        colst[0, y, i, 0] = peak
        colst[0, y, i, 1] = colst0[0, i, 1] * jnp.exp2(m0 - peak) + colst0[1, i, 1] * jnp.exp2(
            m1 - peak
        )
    kcopies = []
    for d in (1, 2, 3):
        kcopies.append(rc(colst.at[0, y], colst.at[0, y], css.at[d - 1], csv.at[d - 1], ypeer[d]))
        kcopies.append(rc(colst.at[0, y], colst.at[1, y], css.at[d + 2], csv.at[d + 2], yopeer[d]))
    kcopies.append(rc(colst.at[0, y], colst.at[1, y], css.at[6], csv.at[6], part_g))
    for c in kcopies:
        c.start()

    for c in rcopies:
        c.wait()
    peak = rowst[0, 0]
    for n in range(1, 8):
        peak = jnp.maximum(peak, rowst[n, 0])
    tot = jnp.zeros_like(peak)
    for n in range(8):
        tot = tot + rowst[n, 1] * jnp.exp2(rowst[n, 0] - peak)
    row_lse = peak + jnp.log2(tot)
    ml[...] = row_lse

    for c in kcopies:
        c.wait()
    for i in range(2):
        peak = colst[0, 0, i, 0]
        for n in range(4):
            peak = jnp.maximum(jnp.maximum(peak, colst[0, n, i, 0]), colst[1, n, 1 - i, 0])
        tot = jnp.zeros_like(peak)
        for n in range(4):
            a0 = colst[0, n, i, 1] * jnp.exp2(colst[0, n, i, 0] - peak)
            a1 = colst[1, n, 1 - i, 1] * jnp.exp2(colst[1, n, 1 - i, 0] - peak)
            tot = tot + (a0 + a1)
        cl_t[pl.ds(i * 8, 8), :] = peak + jnp.log2(tot)

    pacc[...] = jnp.zeros_like(pacc)
    start0 = (x * 4 + z) * 1024
    start1 = (xo * 4 + z) * 1024

    def dlogit(a, carry):
        r = pl.ds(pl.multiple_of(a * 128, 128), 128)
        rl = jnp.broadcast_to(ml[pl.ds(a, 1), :], (128, 128)).T
        pos = jnp.broadcast_to(posbuf[h, pl.ds(k * 8 + a, 1), :], (128, 128)).T
        lane = lax.broadcasted_iota(jnp.int32, (128, 128), 1)
        acc = jnp.zeros((8, 128), F32)
        for c in range(16):
            base = (start0 if c < 8 else start1) + (c % 8) * 128
            off = pos - base
            v = s_buf[c, r, :]
            hot = off == lane
            p = jnp.exp2(v - rl) + jnp.exp2(v - cl_t[pl.ds(c, 1), :])
            p = jnp.where(hot, p - 2.0, p)
            acc = acc + jnp.sum(jnp.where(hot, v, 0.0).reshape(16, 8, 128), axis=0)
            p = p.astype(BF16)
            dl[r, c * 128:(c + 1) * 128] = p
            dlt[c * 128:(c + 1) * 128, r] = p.T
        pacc[...] += acc
        return carry

    lax.fori_loop(0, 8, dlogit, 0)

    sub = lax.broadcasted_iota(jnp.int32, (8, 128), 0)
    part = jnp.where(sub == me_row, row_lse, 0.0) + jnp.where(sub == y * 2 + k, cl_t[0:8, :], 0.0)
    loss_part = (part - 2.0 * pacc[...]) * LN2
    loss_now = {}

    def loss_begin(n, v, peers, slot, mine):
        lossbuf[slot + mine] = v
        cs = []
        for i, to in enumerate(peers):
            sem = slot + i
            dst = slot + (mine if len(peers) > 1 else 1)
            cs.append(rc(lossbuf.at[slot + mine], lossbuf.at[dst], ls.at[sem], lv.at[sem], to))
        for c in cs:
            c.start()
        loss_now[n] = cs

    def loss_end(n, slot, count):
        for c in loss_now[n]:
            c.wait()
        v = [lossbuf[slot + i] for i in range(count)]
        return v[0] + v[1] if count == 2 else (v[0] + v[1]) + (v[2] + v[3])

    zall, yall = [list(p.values()) for p in (zpeer, ypeer)]

    def grad_q(t):
        g = jnp.concatenate(
            [jnp.concatenate([gbuf[xj[t], m, i] for i in range(4)], axis=0) for m in range(2)],
            axis=1,
        )
        o = jnp.dot(dl[...], g, preferred_element_type=F32)
        for i in range(4):
            s_buf[i * 4 + t] = o[:, i * 128:(i + 1) * 128]

    def grad_g(t, rels, kk):
        cols = []
        for rel in rels:
            i = mod4(y + rel)
            j = jnp.where(i == x, 0, jnp.where(i == xo, 1, jnp.where(i == xi, 2, 3)))
            cols += [qbuf[2 * kk, j], qbuf[2 * kk + 1, j]]
        q = jnp.concatenate(cols, axis=1)
        return jnp.dot(dlt[t * 512:(t + 1) * 512, :], q, preferred_element_type=F32)

    sent = []

    class Side:
        def __init__(self, get, rows, bufs, sems, plus, minus, partner):
            self.get, self.rows, self.bufs, self.sems = get, rows, bufs, sems
            self.plus, self.minus, self.partner = plus, minus, partner
            self.msgs = {}

        def send(self, halves, slot, to):
            s, r, ss, sr = self.bufs
            cs, cv, vs, vv = self.sems
            src = slot
            if slot >= R4:
                src = slot - R4 + R1
                for c in self.msgs[src]:
                    c.wait_send()
                sent[:] = [c for c in sent if all(c is not d for d in self.msgs[src])]
            for n, v in enumerate(halves):
                code, sca = encode(v)
                s[src + n] = code
                ss[src + n] = sca
            here, there, n = pl.ds(src, len(halves)), pl.ds(slot, len(halves)), slot
            pair = (
                rc(s.at[here], r.at[there], cs.at[n], cv.at[n], to),
                rc(ss.at[here], sr.at[there], vs.at[n], vv.at[n], to),
            )
            for c in pair:
                c.start()
            sent.extend(pair)
            self.msgs[slot] = pair

        def arrive(self, slot):
            for c in self.msgs[slot]:
                c.wait_recv()

        def val(self, slot):
            return decode(self.bufs[1][slot], self.bufs[3][slot])

        def half(self, rel, t, u):
            return self.get(rel, t, pl.ds(u * self.rows, self.rows))

        def halves(self, rel, t):
            return [self.half(rel, t, u) for u in range(2)]

        def outer(self, t):
            n = (t - 2) * 2
            self.send(self.halves(2, t), R1 + n, self.partner)
            self.send(self.halves(1, t), R3P + n, self.plus)
            self.send(self.halves(3, t), R3M + n, self.minus)

        def inner(self, t):
            n = t * 2
            self.arrive(R1 + n)
            for u, to in ((0, self.plus), (1, self.minus)):
                self.send([self.half(2, t, u) + self.val(R1 + n + u)], R2 + n + u, to)
            self.send([self.half(1, t, 1)], R3PH + n + 1, self.plus)
            self.send([self.half(3, t, 0)], R3MH + n, self.minus)

        def late(self, t):
            n = t * 2
            self.arrive(R2 + n)
            self.send([self.half(1, t, 0) + self.val(R2 + n)], R3PH + n, self.plus)
            self.arrive(R2 + n + 1)
            self.send([self.half(3, t, 1) + self.val(R2 + n + 1)], R3MH + n + 1, self.minus)

        def across(self, t):
            n = (t - 2) * 2
            self.arrive(R3P + n)
            self.arrive(R3M + n)
            self.send(
                [self.half(0, t, u) + self.val(R3P + n + u) + self.val(R3M + n + u)
                 for u in range(2)],
                R4 + n, self.partner,
            )

        def final(self, t, u):
            n = t * 2
            if ("4", t) not in self.msgs:
                self.arrive(R4 + n)
                self.msgs["4", t] = True
            self.arrive(R3PH + n + u)
            self.arrive(R3MH + n + u)
            return (
                (self.half(0, t, u) + self.val(R4 + n + u))
                + (self.val(R3PH + n + u) + self.val(R3MH + n + u))
            )

    qside = Side(
        lambda rel, t, r: s_buf[mod4(z + rel) * 4 + t, r, :], 512,
        (qr_s, qr_r, qr_ss, qr_sr), (qcs, qcv, qss, qsv), zpeer[1], zpeer[3], part_q,
    )
    gside = Side(
        lambda rel, t, r: pg[rel, t, r, :], 256,
        (gr_s, gr_r, gr_ss, gr_sr), (gcs, gcv, gss, gsv), ypeer[1], ypeer[3], part_g,
    )
    order = (2, 1, 3, 0)
    xmsg = {}

    def grad_g_other(t):
        if t < 2:
            for c in xmsg[t + 2]:
                c.wait_send()
        o = grad_g(t, order, 1 - k)
        for n, rel in enumerate(order):
            code, sca = encode(o[:, n * 256:(n + 1) * 256])
            cx_s[t % 2, rel] = code
            cx_ss[t % 2, rel] = sca
        c1 = rc(cx_s.at[t % 2], cx_r.at[t], xs.at[t], xv.at[t], core)
        c2 = rc(cx_ss.at[t % 2], cx_sr.at[t], xss.at[t], xsv.at[t], core)
        c1.start()
        c2.start()
        xmsg[t] = (c1, c2)

    def grad_g_own(t):
        o = grad_g(t, order, k)
        for c in xmsg[t]:
            c.wait_recv()
        for n, rel in enumerate(order):
            pg[rel, t] = o[:, n * 256:(n + 1) * 256] + decode(cx_r[t, rel], cx_sr[t, rel])

    loss_begin(0, loss_part, [core], 0, 0)
    for t in (3, 2):
        grad_g_other(t)
        grad_q(t)
        qside.outer(t)
        grad_g_own(t)
        gside.outer(t)
    loss = loss_end(0, 0, 2)
    loss_begin(1, loss, [part_q], 2, 0)
    grad_g_other(1)
    grad_q(1)
    qside.inner(1)
    qside.across(3)
    loss = loss_end(1, 2, 2)
    loss_begin(2, loss, [part_g], 4, 0)
    grad_g_own(1)
    gside.inner(1)
    gside.across(3)
    loss = loss_end(2, 4, 2)
    loss_begin(3, loss, zall, 6, z)
    grad_g_other(0)
    grad_q(0)
    qside.inner(0)
    qside.late(1)
    loss = loss_end(3, 6, 4)
    loss_begin(4, loss, yall, 10, y)
    grad_g_own(0)
    gside.inner(0)
    gside.late(1)
    qside.across(2)
    gside.across(2)
    loss = loss_end(4, 10, 4)
    loss = jnp.sum(jnp.sum(loss, axis=0, keepdims=True), axis=1, keepdims=True)
    loss_ref[...] = jnp.broadcast_to(loss * (1.0 / 32768.0), (8, 128))
    qside.late(0)
    gside.late(0)
    for t in (1, 0):
        for c in xmsg[t]:
            c.wait_send()

    out_to = dev(xo, y, z, h)
    out_sem = k * 2
    for u in (1, 0):
        code, sca = encode(qside.final(1, u))
        qr_s[OUT + u] = code
        qr_ss[OUT + u] = sca
        for c in (
            rc(qr_s.at[OUT + u], qo_r.at[k, u], qcs.at[NSLOT + u], ov.at[out_sem + u], out_to),
            rc(qr_ss.at[OUT + u], qo_sr.at[k, u], qss.at[NSLOT + u], ovs.at[out_sem + u], out_to),
        ):
            c.start()
            sent.append(c)
    def put_g(n, v):
        r = pl.ds(n * 256, 256)
        gout[r, :] = v
        c = pltpu.make_async_copy(gout.at[r], gg_ref.at[r], osem.at[4 + n])
        c.start()
        return c

    puts = [put_g(2 + u, gside.final(1, u)) for u in (1, 0)]
    for u in (1, 0):
        qout[k, u] = qside.final(0, u)
    rows_k = pl.ds(k * 2, 2)
    out_core = rc(qout.at[k], qg_ref.at[rows_k], ms.at[7], mv.at[5 + k], core)
    out_here = pltpu.make_async_copy(qout.at[k], qg_ref.at[rows_k], osem.at[8])

    @pl.when(h == k)
    def _():
        out_here.start()

    @pl.when(h != k)
    def _():
        out_core.start()

    puts += [put_g(u, gside.final(0, u)) for u in (1, 0)]

    @pl.when(h == k)
    def _():
        out_here.wait()
        rc(qout.at[k], qg_ref.at[pl.ds((1 - k) * 2, 2)], ms.at[7], mv.at[6 - k], core).wait_recv()
        q1c.wait_send()

    @pl.when(h != k)
    def _():
        out_core.wait_send()
        moves = []
        for u in (1, 0):
            for kk in range(2):
                rc(qr_s.at[OUT], qo_r.at[kk, u], qcs.at[OUT], ov.at[kk * 2 + u],
                   out_to).wait_recv()
                rc(qr_ss.at[OUT], qo_sr.at[kk, u], qss.at[OUT], ovs.at[kk * 2 + u],
                   out_to).wait_recv()
                qout[kk, u] = decode(qo_r[kk, u], qo_sr[kk, u])
                c = pltpu.make_async_copy(
                    qout.at[kk, u], qg_ref.at[kk * 2 + u], osem.at[kk * 2 + u]
                )
                c.start()
                moves.append(c)
        for c in moves:
            c.wait()
        for c in q1o:
            c.wait_send()

    for c in puts:
        c.wait()
    pos_copy.wait_send()
    for m in (qm, gm):
        for c in m.values():
            c.wait_send()
    for c in ecopies + sent:
        c.wait_send()


def hand_on(loss_in, qg_in, gg_in, loss_out, qg_out, gg_out, qv, gv, sem):
    ins, outs = [], []
    for i in range(4):
        a, b = pl.ds(i * 512, 512), pl.ds(i * 256, 256)
        for n, (src, mid, dst, r) in enumerate(((qg_in, qv, qg_out, a), (gg_in, gv, gg_out, b))):
            ins.append(pltpu.make_async_copy(src.at[r], mid.at[r], sem.at[0, i, n]))
            outs.append(pltpu.make_async_copy(mid.at[r], dst.at[r], sem.at[1, i, n]))
    for c in ins:
        c.start()
    loss_out[0, 0] = loss_in[0, 0]
    for c, d in zip(ins, outs):
        c.wait()
        d.start()
    for c in outs:
        c.wait()


def on_device(query_embed, gist_embed, positive):
    pos = positive.reshape(16, 128)
    vm, dma = pltpu.VMEM, pltpu.SemaphoreType.DMA
    scratch = [
        vm((4, 4, 1024, 128), BF16),
        vm((4, 2, 4, 512, 256), BF16),
        vm((16, 1024, 128), F32),
        vm((1024, 2048), BF16),
        vm((2048, 1024), BF16),
        vm((2, 16, 128), jnp.int32),
        vm((8, 128), F32),
        vm((8, 128), F32),
        vm((16, 8, 128), F32),
        vm((16, 8, 128), F32),
        vm((8, 2, 8, 128), F32),
        vm((2, 2, 2, 8, 128), F32),
        vm((2, 4, 2, 2, 8, 128), F32),
        vm((16, 128), F32),
        vm((8, 128), F32),
        vm((OUT + 2, 512, 128), I16),
        vm((NSLOT, 512, 128), I16),
        vm((OUT + 2, 8, 128), F32),
        vm((NSLOT, 8, 128), F32),
        vm((OUT, 256, 256), I16),
        vm((NSLOT, 256, 256), I16),
        vm((OUT, 8, 256), F32),
        vm((NSLOT, 8, 256), F32),
        vm((2, 4, 512, 256), I16),
        vm((4, 4, 512, 256), I16),
        vm((2, 4, 8, 256), F32),
        vm((4, 4, 8, 256), F32),
        vm((4, 4, 512, 256), F32),
        vm((2, 2, 512, 128), F32),
        vm((1024, 256), F32),
        vm((2, 2, 512, 128), I16),
        vm((2, 2, 8, 128), F32),
        vm((14, 8, 128), F32),
        dma((NGATHER,)), dma((NGATHER,)),
        dma((NGATHER,)), dma((NGATHER,)),
        dma((4, 4, 2)), dma((4, 4, 2)),
        dma((8,)), dma((8,)),
        dma((7,)), dma((7,)),
        dma((7,)), dma((7,)),
        dma((14,)), dma((14,)),
        dma((NSLOT + 2,)), dma((NSLOT,)),
        dma((NSLOT + 2,)), dma((NSLOT,)),
        dma((NSLOT,)), dma((NSLOT,)),
        dma((NSLOT,)), dma((NSLOT,)),
        dma((4,)), dma((4,)),
        dma((4,)), dma((4,)),
        dma((4,)), dma((4,)),
        dma((4,)),
        dma((9,)),
    ]
    loss, qg, gg = pl.pallas_call(
        kernel,
        out_shape=[
            jax.ShapeDtypeStruct((8, 128), F32),
            jax.ShapeDtypeStruct((4, 512, 128), F32),
            jax.ShapeDtypeStruct((1024, 256), F32),
        ],
        in_specs=[
            pl.BlockSpec(memory_space=pl.ANY),
            pl.BlockSpec(memory_space=pl.ANY),
            pl.BlockSpec(memory_space=pltpu.VMEM),
        ],
        out_specs=[
            pl.BlockSpec(memory_space=pltpu.VMEM),
            pl.BlockSpec(memory_space=pl.ANY),
            pl.BlockSpec(memory_space=pl.ANY),
        ],
        scratch_shapes=scratch,
        compiler_params=pltpu.CompilerParams(
            collective_id=0, has_side_effects=True, vmem_limit_bytes=63 * 2**20
        ),
    )(query_embed, gist_embed, pos)
    loss, qg, gg = pl.pallas_call(
        hand_on,
        out_shape=[
            jax.ShapeDtypeStruct((1, 1), F32),
            jax.ShapeDtypeStruct((2048, 128), F32),
            jax.ShapeDtypeStruct((1024, 256), F32),
        ],
        in_specs=[
            pl.BlockSpec(memory_space=pltpu.VMEM),
            pl.BlockSpec(memory_space=pl.ANY),
            pl.BlockSpec(memory_space=pl.ANY),
        ],
        out_specs=[
            pl.BlockSpec(memory_space=pltpu.SMEM),
            pl.BlockSpec(memory_space=pl.ANY),
            pl.BlockSpec(memory_space=pl.ANY),
        ],
        scratch_shapes=[vm((2048, 128), F32), vm((1024, 256), F32), dma((2, 4, 2))],
    )(loss, qg.reshape(2048, 128), gg)
    return loss[0, 0], qg, gg


def solution(mesh):
    in_specs = (P("row", "col"), P("col", "row"), P("row"))
    out_specs = (P(), P("row", "col"), P("col", "row"))
    return jax.shard_map(
        on_device, mesh=mesh, in_specs=in_specs, out_specs=out_specs, check_vma=False
    )
```

```python
import functools
import math

import jax
import jax.numpy as jnp
from jax import lax
from jax.experimental import pallas as pl
from jax.experimental.pallas import tpu as pltpu
from jax.sharding import PartitionSpec as P

D = 2048
MESH = pl.DeviceIdType.MESH
LOG2E = 1.4426950408889634
LN2 = 0.6931471805599453
F32 = jnp.float32
BF16 = jnp.bfloat16
I16 = jnp.int16
TOP = 14.98

A, BP, BM, C, DD = 0, 4, 12, 20, 24
R1, R3P, R3M, R2, R3PH, R3MH, R4, NSLOT = 0, 4, 8, 12, 16, 20, 24, 28
OUT = R4


def where_am_i():
    row = lax.axis_index("row")
    col = lax.axis_index("col")
    return lax.div(col, 4), lax.div(row, 2), lax.rem(col, 4), lax.rem(row, 2)


def mod4(v):
    return lax.rem(v + 8, 4)


def encode(x):
    rows, cols = x.shape
    x3 = x.reshape(rows // 8, 8, cols)
    top = jnp.maximum(jnp.max(jnp.abs(x3), axis=0), 1e-30)
    e = jnp.ceil(jnp.log2(top) * 64.0)
    code = jnp.round(x3 * jnp.exp2(TOP - e * (1.0 / 64.0))[None]).reshape(rows, cols)
    return code.astype(jnp.int32).astype(I16), jnp.concatenate([e, e]).astype(jnp.int32).astype(I16)


def put(ref, v):
    rows = v.shape[0]
    code, e = encode(v)
    ref[pl.ds(0, rows), :] = code
    ref[pl.ds(rows, 16), :] = e


def decode(ref, rows):
    e = ref[pl.ds(rows, 16), :].astype(jnp.int32).astype(F32)[:8]
    x = ref[pl.ds(0, rows), :].astype(jnp.int32).astype(F32)
    x3 = x.reshape(rows // 8, 8, x.shape[1]) * jnp.exp2(e * (1.0 / 64.0) - TOP)[None]
    return x3.reshape(x.shape)


def kernel(
    q_ref, g_ref, pos_ref, loss_ref, qg_ref, gg_ref,
    qbuf, gbuf, s_buf, dl, dlt, posbuf,
    ml, sl, mc, sc, rowst, colst0, colst, cl_t, pacc,
    qr_s, qr_r, gr_s, gr_r, cx_s, cx_r, pg, qout, qo_r, lossbuf,
    qs, qv, gs, gv, es, ev, ms, mv, rs, rv, cs_, cv_, ls, lv, xs, xv, ov, lsem, osem,
):
    x, y, z, k = where_am_i()
    h = lax.div(x, 2)
    e = lax.rem(x, 2)
    xi = x + 1 - 2 * e
    xo = 3 - x
    xio = 3 - xi
    xj = [x, xo, xi, xio]

    def dev(xx, yy, zz, kk):
        return (yy * 2 + kk, xx * 4 + zz)

    core = dev(x, y, z, 1 - k)
    part_q = dev(xi, y, z, k)
    part_g = dev(xo, y, z, k)
    part_g2 = dev(xo, y, z, 1 - k)
    zpeer = {d: dev(x, y, mod4(z + d), k) for d in (1, 2, 3)}
    ypeer = {d: dev(x, mod4(y + d), z, k) for d in (1, 2, 3)}
    zipeer = {d: dev(xi, y, mod4(z + d), k) for d in (1, 2, 3)}
    yopeer = {d: dev(xo, mod4(y + d), z, k) for d in (1, 2, 3)}
    everyone = [core, part_q, part_g, part_g2]
    for group in (zpeer, ypeer, zipeer, yopeer):
        everyone += list(group.values())

    barrier = pltpu.get_barrier_semaphore()
    for other in everyone:
        pl.semaphore_signal(barrier, inc=1, device_id=other, device_id_type=MESH)

    def rc(src, dst, s, v, to):
        return pltpu.make_async_remote_copy(
            src_ref=src, dst_ref=dst, send_sem=s, recv_sem=v, device_id=to, device_id_type=MESH
        )

    gl = [
        pltpu.make_async_copy(g_ref.at[pl.ds(t * 512, 512)], gbuf.at[y, k, t], lsem.at[t])
        for t in range(2)
    ]
    for c in gl:
        c.start()
    here = pltpu.make_async_copy(q_ref.at[pl.ds(k * 1024, 1024)], qbuf.at[z, 0], lsem.at[2])
    posc = pltpu.make_async_copy(pos_ref, posbuf.at[k], lsem.at[3])
    posc.start()

    @pl.when(h == k)
    def _():
        here.start()

    pl.semaphore_wait(barrier, len(everyone))

    pos_copy = rc(pos_ref, posbuf.at[k], ms.at[0], mv.at[0], core)
    pos_copy.start()
    q1c = rc(q_ref.at[pl.ds((1 - k) * 1024, 1024)], qbuf.at[z, 0], ms.at[1], mv.at[1], core)
    q1o = [
        rc(q_ref.at[pl.ds(kk * 1024 + u * 512, 512)], qbuf.at[z, 1, pl.ds(u * 512, 512)],
           ms.at[2], mv.at[2 + u], dev(xo, y, z, kk))
        for u in range(2) for kk in range(2)
    ]

    @pl.when(h == k)
    def _():
        q1c.start()

    @pl.when(h != k)
    def _():
        for c in q1o:
            c.start()

    def qp(i, t, u):
        return qbuf.at[i, t, pl.ds(u * 512, 512)]

    def gp(i, t, u):
        return gbuf.at[i, k, t, pl.ds(u * 256, 256)]

    def ring(buf, r, sems, semv, plus, minus, partner):
        def msg(i, t, u, t2, idx, to):
            return rc(buf(i, t, u), buf(i, t2, u), sems.at[0], semv.at[idx], to)

        before, after, far = mod4(r - 1), mod4(r + 1), mod4(r + 2)
        m = {}
        for t in range(4):
            for u in range(2):
                n = t * 2 + u
                if t < 2:
                    m["a", t, u] = msg(r, t, u, t + 2, A + n, partner)
                    m["d", t, u] = msg(far, t, u, t + 2, DD + n, partner)
                    m["c", t, u] = msg(before if u == 0 else after, t, u, t, C + n,
                                       plus if u == 0 else minus)
                m["p", t, u] = msg(r, t, u, t, BP + n, plus)
                m["m", t, u] = msg(r, t, u, t, BM + n, minus)
        return m

    qm = ring(qp, z, qs, qv, zpeer[1], zpeer[3], part_q)
    gm = ring(gp, y, gs, gv, ypeer[1], ypeer[3], part_g)
    yb, ya, yf = mod4(y - 1), mod4(y + 1), mod4(y + 2)

    def start_core(i, t, u):
        rc(gp(i, t, u), gp(i, t, u), es.at[max(t - 1, 0)], ev.at[max(t - 1, 0)], core).start()

    def both(m, t, first):
        u = first
        m["p", t, u].start()
        m["m", t, 1 - u].start()

    def on(m, t):
        m["p", t, 0].wait_recv()
        m["c", t, 0].start()
        m["m", t, 1].wait_recv()
        m["c", t, 1].start()

    for c in gl:
        c.wait()
    both(gm, 0, 0)
    both(gm, 0, 1)
    for t in range(2):
        for u in range(2):
            gm["a", t, u].start()
    both(gm, 1, 0)

    @pl.when(h == k)
    def _():
        here.wait()

    @pl.when(h != k)
    def _():
        q1c.wait_recv()

    both(qm, 0, 0)
    both(qm, 0, 1)
    for u in range(2):
        qm["a", 0, u].start()
    for t in range(2):
        for u in range(2):
            start_core(y, t, u)
    on(gm, 0)
    on(qm, 0)
    both(gm, 1, 1)
    q1o[0].wait_recv()
    q1o[2].wait_recv()
    both(qm, 1, 0)
    qm["a", 1, 0].start()
    both(qm, 1, 1)
    qm["a", 1, 1].start()
    start_core(yb, 0, 0)
    start_core(ya, 0, 1)
    gm["p", 0, 1].wait_recv()
    start_core(yb, 0, 1)
    gm["m", 0, 0].wait_recv()
    start_core(ya, 0, 0)
    on(gm, 1)
    start_core(yb, 1, 0)
    start_core(ya, 1, 1)
    for u in range(2):
        gm["c", 0, u].wait_recv()
        gm["d", 0, u].start()
        start_core(yf, 0, u)
        qm["c", 0, u].wait_recv()
        qm["d", 0, u].start()
    on(qm, 1)
    for u in range(2):
        gm["a", 0, u].wait_recv()
        gm["p", 2, u].start()
        gm["m", 2, u].start()
        start_core(y, 2, u)
        qm["a", 0, u].wait_recv()
        qm["p", 2, u].start()
        qm["m", 2, u].start()
    gm["p", 1, 1].wait_recv()
    start_core(yb, 1, 1)
    gm["m", 1, 0].wait_recv()
    start_core(ya, 1, 0)
    for u in range(2):
        qm["a", 1, u].wait_recv()
        qm["p", 3, u].start()
        qm["m", 3, u].start()
        gm["a", 1, u].wait_recv()
        gm["p", 3, u].start()
        gm["m", 3, u].start()
        start_core(y, 3, u)
    for u in range(2):
        gm["c", 1, u].wait_recv()
        gm["d", 1, u].start()
        start_core(yf, 1, u)
        qm["c", 1, u].wait_recv()
        qm["d", 1, u].start()
    def all_core(n, mine):
        r = gbuf.at[:, mine, pl.ds(0, 2) if n == 0 else pl.ds(n + 1, 1)]
        return rc(r, r, es.at[n], ev.at[n], core)

    scale = LOG2E / math.sqrt(D)

    def logits(t, js, add):
        g = jnp.concatenate([gbuf[xj[j], m, t] for j in js for m in range(2)], axis=1)
        q = jnp.concatenate(
            [qbuf[2 * m + u, j] for j in js for m in range(2) for u in range(2)], axis=1
        )
        s = lax.dot_general(q, g, (((1,), (1,)), ((), ())), preferred_element_type=F32)
        s = s * scale
        for u in range(4):
            v = s[:, u * 128:(u + 1) * 128]
            s_buf[t * 4 + u] = s_buf[t * 4 + u] + v if add else v

    def queries_there(t):
        for u in range(2):
            if t >= 2 or u == 1:
                qm["p", t, u].wait_recv()
            if t >= 2 or u == 0:
                qm["m", t, u].wait_recv()
            if t >= 2:
                qm["d", t - 2, u].wait_recv()

    queries_there(0)
    queries_there(1)
    all_core(0, 1 - k).wait_recv()
    logits(0, (0, 1), False)
    logits(1, (0, 1), False)
    for t in range(2, 4):
        for u in range(2):
            gm["p", t, u].wait_recv()
            start_core(yb, t, u)
            gm["m", t, u].wait_recv()
            start_core(ya, t, u)
        if t == 2:
            for u in range(2):
                gm["d", 0, u].wait_recv()
                start_core(yf, 2, u)
            queries_there(2)
            all_core(1, 1 - k).wait_recv()
            logits(0, (2,), True)
            logits(1, (2,), True)
            logits(2, (0, 1, 2), False)
    for u in range(2):
        gm["d", 1, u].wait_recv()
        start_core(yf, 3, u)
    queries_there(3)
    posc.wait()
    pos_copy.wait_recv()

    def stats(t):
        for u in range(4):
            c = t * 4 + u
            v3 = s_buf[c].reshape(128, 8, 128)
            top = jnp.max(v3, axis=0)
            mc[c] = top
            sc[c] = jnp.sum(jnp.exp2(v3 - top[None]), axis=0)
        for b in range(2):
            for d in range(4):
                r, rb = pl.ds(b * 512 + d * 128, 128), pl.ds(d * 128, 128)
                v = [s_buf[t * 4 + u, r, :] for u in range(4)]
                top = jnp.maximum(jnp.maximum(v[0], v[1]), jnp.maximum(v[2], v[3]))
                if t > 0:
                    old = qout[0, b, rb, :]
                    top = jnp.maximum(old, top)
                e = [jnp.exp2(w - top) for w in v]
                total = (e[0] + e[1]) + (e[2] + e[3])
                if t > 0:
                    total = total + qout[1, b, rb, :] * jnp.exp2(old - top)
                qout[0, b, rb, :] = top
                qout[1, b, rb, :] = total

    for t in range(3):
        logits(t, (3,), True)
        if t > 0:
            stats(t - 1)
    all_core(2, 1 - k).wait_recv()
    logits(3, (0, 1, 2, 3), False)
    stats(2)
    stats(3)
    for a in range(8):
        rb = pl.ds((a % 4) * 128, 128)
        tt = qout[0, a // 4, rb, :].T
        peak = jnp.max(tt, axis=0, keepdims=True)
        total = qout[1, a // 4, rb, :].T
        ml[pl.ds(a, 1), :] = peak
        sl[pl.ds(a, 1), :] = jnp.sum(total * jnp.exp2(tt - peak), axis=0, keepdims=True)

    for c in range(16):
        peak = jnp.max(mc[c], axis=0, keepdims=True)
        one = jnp.sum(sc[c] * jnp.exp2(mc[c] - peak), axis=0, keepdims=True)
        colst0[0, c // 8, 0, pl.ds(c % 8, 1), :] = peak
        colst0[0, c // 8, 1, pl.ds(c % 8, 1), :] = one
    ccopy = rc(colst0.at[0], colst0.at[1], ms.at[3], mv.at[4], core)
    ccopy.start()

    me_row = e * 4 + z
    rowst[me_row, 0] = ml[...]
    rowst[me_row, 1] = sl[...]
    for to in list(zpeer.values()) + list(zipeer.values()) + [part_q]:
        rc(rowst.at[me_row], rowst.at[me_row], rs, rv, to).start()
    rall = rc(rowst.at[pl.ds(0, 7)], rowst.at[pl.ds(0, 7)], rs, rv, part_q)

    ccopy.wait()
    for i in range(2):
        m0, m1 = colst0[0, i, 0], colst0[1, i, 0]
        peak = jnp.maximum(m0, m1)
        colst[y, i, 0] = peak
        colst[y, i, 1] = colst0[0, i, 1] * jnp.exp2(m0 - peak) + colst0[1, i, 1] * jnp.exp2(
            m1 - peak
        )
    for to in ypeer.values():
        rc(colst.at[y], colst.at[y], cs_, cv_, to).start()
    for to in list(yopeer.values()) + [part_g]:
        rc(colst.at[y], colst.at[4 + y], cs_, cv_, to).start()
    kall = rc(colst.at[pl.ds(0, 7)], colst.at[pl.ds(0, 7)], cs_, cv_, part_g)

    rall.wait()
    peak = rowst[0, 0]
    for n in range(1, 8):
        peak = jnp.maximum(peak, rowst[n, 0])
    tot = jnp.zeros_like(peak)
    for n in range(8):
        tot = tot + rowst[n, 1] * jnp.exp2(rowst[n, 0] - peak)
    row_lse = peak + jnp.log2(tot)
    ml[...] = row_lse

    kall.wait()
    for i in range(2):
        peak = colst[0, i, 0]
        for n in range(4):
            peak = jnp.maximum(jnp.maximum(peak, colst[n, i, 0]), colst[4 + n, 1 - i, 0])
        tot = jnp.zeros_like(peak)
        for n in range(4):
            a0 = colst[n, i, 1] * jnp.exp2(colst[n, i, 0] - peak)
            a1 = colst[4 + n, 1 - i, 1] * jnp.exp2(colst[4 + n, 1 - i, 0] - peak)
            tot = tot + (a0 + a1)
        cl_t[pl.ds(i * 8, 8), :] = peak + jnp.log2(tot)

    for a in range(8):
        r = pl.ds((a % 4) * 128, 128)
        qout[0, a // 4, r, :] = jnp.broadcast_to(ml[pl.ds(a, 1), :], (128, 128)).T
        pos = posbuf[h, pl.ds(k * 8 + a, 1), :].astype(F32)
        qout[1, a // 4, r, :] = jnp.broadcast_to(pos, (128, 128)).T
    lane = lax.broadcasted_iota(jnp.int32, (1, 128), 1)
    first = [(x * 4 + z) * 1024, (xo * 4 + z) * 1024]

    def dlogit(t):
        acc = jnp.zeros((8, 128), F32)
        for u in range(4):
            c = t * 4 + u
            cl = cl_t[pl.ds(c, 1), :]
            own = (lane + (first[c // 8] + (c % 8) * 128)).astype(F32)
            for a in range(8):
                r, rb = pl.ds(a * 128, 128), pl.ds((a % 4) * 128, 128)
                v = s_buf[c, r, :]
                hot = jnp.where(qout[1, a // 4, rb, :] == own, 2.0, 0.0)
                p = jnp.exp2(v - qout[0, a // 4, rb, :]) + jnp.exp2(v - cl) - hot
                acc = acc + jnp.sum((v * hot).reshape(16, 8, 128), axis=0)
                p = p.astype(BF16)
                dl[r, c * 128:(c + 1) * 128] = p
                dlt[c * 128:(c + 1) * 128, r] = p.T
        pacc[t] = acc

    dlogit(3)

    sub = lax.broadcasted_iota(jnp.int32, (8, 128), 0)
    lse_part = jnp.where(sub == me_row, row_lse, 0.0) + jnp.where(sub == y * 2 + k, cl_t[0:8, :], 0.0)
    loss_now = {}

    def loss_begin(n, v, peers, slot, mine):
        lossbuf[slot + mine] = v
        dst = slot + (mine if len(peers) > 1 else 1)
        for to in peers:
            rc(lossbuf.at[slot + mine], lossbuf.at[dst], ls.at[n], lv.at[n], to).start()
        got = lossbuf.at[pl.ds(slot, len(peers))]
        loss_now[n] = rc(got, got, ls.at[n], lv.at[n], peers[0])

    def loss_end(n, slot, count):
        loss_now[n].wait()
        v = [lossbuf[slot + i] for i in range(count)]
        return v[0] + v[1] if count == 2 else (v[0] + v[1]) + (v[2] + v[3])

    zall, yall = [list(p.values()) for p in (zpeer, ypeer)]

    def grad_q(t):
        g = jnp.concatenate(
            [jnp.concatenate([gbuf[xj[t], m, i] for i in range(4)], axis=0) for m in range(2)],
            axis=1,
        )
        o = jnp.dot(dl[...], g, preferred_element_type=F32)
        for i in range(4):
            s_buf[i * 4 + t] = o[:, i * 128:(i + 1) * 128]

    def grad_g(t, rels, kk):
        cols = []
        for rel in rels:
            i = mod4(y + rel)
            j = jnp.where(i == x, 0, jnp.where(i == xo, 1, jnp.where(i == xi, 2, 3)))
            cols += [qbuf[2 * kk, j], qbuf[2 * kk + 1, j]]
        q = jnp.concatenate(cols, axis=1)
        return jnp.dot(dlt[t * 512:(t + 1) * 512, :], q, preferred_element_type=F32)

    for m, sem, ref in ((qm, qs, qbuf.at[:, :, pl.ds(0, 896)]),
                        (gm, gs, gbuf.at[:, k, :, pl.ds(0, 448)])):
        rc(ref, ref, sem.at[0], qv.at[0], core).wait_send()
    for n in range(3):
        all_core(n, k).wait_send()

    class Side:
        def __init__(self, get, rows, bufs, sems, plus, minus, partner):
            self.get, self.rows, self.bufs, self.sems = get, rows, bufs, sems
            self.plus, self.minus, self.partner = plus, minus, partner
            self.msgs = {}

        def send(self, *many):
            s, r = self.bufs
            cs, cv = self.sems
            copies = []
            for halves, slot, to in many:
                src, sem = slot, 1
                if slot >= R4:
                    src = slot - R4 + R1
                    self.msgs[src].wait_send()
                elif slot < R3P:
                    sem = 2 + (slot - R1) // 2
                here, there = pl.ds(src, len(halves)), pl.ds(slot, len(halves))
                c = rc(s.at[here], r.at[there], cs.at[sem], cv.at[slot], to)
                self.msgs[slot] = c
                copies.append(c)
                for n, v in enumerate(halves):
                    put(s.at[src + n], v)
            for c in copies:
                c.start()

        def sent(self, count):
            r = self.bufs[1].at[pl.ds(0, count)]
            rc(r, r, self.sems[0].at[1], self.sems[1].at[0], self.plus).wait_send()

        def arrive(self, slot):
            self.msgs[slot].wait_recv()

        def val(self, slot):
            return decode(self.bufs[1].at[slot], self.rows)

        def half(self, rel, t, u):
            return self.get(rel, t, pl.ds(u * self.rows, self.rows))

        def halves(self, rel, t):
            return [self.half(rel, t, u) for u in range(2)]

        def outer(self, t):
            n = (t - 2) * 2
            self.send(
                (self.halves(2, t), R1 + n, self.partner),
                (self.halves(1, t), R3P + n, self.plus),
                (self.halves(3, t), R3M + n, self.minus),
            )

        def inner(self, t):
            n = t * 2
            self.arrive(R1 + n)
            far = [self.half(2, t, u) + self.val(R1 + n + u) for u in range(2)]
            self.send(
                ([far[0]], R2 + n, self.plus),
                ([far[1]], R2 + n + 1, self.minus),
                ([self.half(1, t, 1)], R3PH + n + 1, self.plus),
                ([self.half(3, t, 0)], R3MH + n, self.minus),
            )

        def late(self, t):
            n = t * 2
            self.arrive(R2 + n)
            self.arrive(R2 + n + 1)
            self.send(
                ([self.half(1, t, 0) + self.val(R2 + n)], R3PH + n, self.plus),
                ([self.half(3, t, 1) + self.val(R2 + n + 1)], R3MH + n + 1, self.minus),
            )

        def across(self, t):
            n = (t - 2) * 2
            self.arrive(R3P + n)
            self.arrive(R3M + n)
            v = [
                self.half(0, t, u) + self.val(R3P + n + u) + self.val(R3M + n + u)
                for u in range(2)
            ]
            self.send((v, R4 + n, self.partner))

        def final(self, t, u):
            n = t * 2
            if ("4", t) not in self.msgs:
                self.arrive(R4 + n)
                self.msgs["4", t] = True
            self.arrive(R3PH + n + u)
            self.arrive(R3MH + n + u)
            return (
                (self.half(0, t, u) + self.val(R4 + n + u))
                + (self.val(R3PH + n + u) + self.val(R3MH + n + u))
            )

    qside = Side(
        lambda rel, t, r: s_buf[mod4(z + rel) * 4 + t, r, :], 512,
        (qr_s, qr_r), (qs, qv), zpeer[1], zpeer[3], part_q,
    )
    gside = Side(
        lambda rel, t, r: pg[rel, t, r, :], 256,
        (gr_s, gr_r), (gs, gv), ypeer[1], ypeer[3], part_g,
    )
    order = (2, 1, 3, 0)
    xmsg = {}

    def grad_g_other(t, beside=None, *args):
        if t < 2:
            xmsg[t + 2].wait_send()
        o = grad_g(t, order, 1 - k)
        if beside is not None:
            beside(*args)
        for n, rel in enumerate(order):
            put(cx_s.at[t % 2, rel], o[:, n * 256:(n + 1) * 256])
        xmsg[t] = rc(cx_s.at[t % 2], cx_r.at[t], xs.at[t % 2], xv.at[t], core)
        xmsg[t].start()

    def grad_g_own(t):
        o = grad_g(t, order, k)
        for n, rel in enumerate(order):
            pg[rel, t] = o[:, n * 256:(n + 1) * 256]

    def grad_g_sum(t):
        xmsg[t].wait_recv()
        for rel in order:
            pg[rel, t] += decode(cx_r.at[t, rel], 512)

    grad_g_other(3, dlogit, 0)
    grad_g_own(3)
    dlogit(1)
    dlogit(2)
    grad_q(3)
    qside.outer(3)
    grad_g_sum(3)
    gside.outer(3)
    hits = (pacc[0] + pacc[1]) + (pacc[2] + pacc[3])
    loss_begin(0, (lse_part - hits) * LN2, [core], 0, 0)
    grad_g_other(2)
    grad_q(2)
    qside.outer(2)
    grad_g_own(2)
    grad_g_sum(2)
    gside.outer(2)
    loss = loss_end(0, 0, 2)
    loss_begin(1, loss, [part_q], 2, 0)
    grad_g_other(1)
    grad_q(1)
    qside.inner(1)
    qside.across(3)
    loss = loss_end(1, 2, 2)
    loss_begin(2, loss, [part_g], 4, 0)
    grad_g_own(1)
    grad_g_sum(1)
    gside.inner(1)
    gside.across(3)
    loss = loss_end(2, 4, 2)
    loss_begin(3, loss, zall, 6, z)
    grad_g_other(0)
    grad_q(0)
    qside.inner(0)
    qside.late(1)
    loss = loss_end(3, 6, 4)
    loss_begin(4, loss, yall, 10, y)
    grad_g_own(0)
    grad_g_sum(0)
    gside.inner(0)
    gside.late(1)
    qside.across(2)
    gside.across(2)
    loss = loss_end(4, 10, 4)
    loss = jnp.sum(jnp.sum(loss, axis=0, keepdims=True), axis=1, keepdims=True)
    loss_ref[...] = jnp.broadcast_to(loss * (1.0 / 32768.0), (8, 128))
    qside.late(0)
    gside.late(0)
    for t in (1, 0):
        xmsg[t].wait_send()

    out_to = dev(xo, y, z, h)
    out_sem = k * 2
    for u in (1, 0):
        put(qr_s.at[OUT + u], qside.final(1, u))
        rc(qr_s.at[OUT + u], qo_r.at[k, u], qs.at[1], ov.at[out_sem + u], out_to).start()

    def put_g(t, u):
        r = pl.ds(u * 256, 256)
        pg[0, t, r, :] = gside.final(t, u)
        n = t * 2 + u
        c = pltpu.make_async_copy(pg.at[0, t, r], gg_ref.at[pl.ds(n * 256, 256)], osem.at[4 + n])
        c.start()
        return c

    puts = [put_g(1, u) for u in (1, 0)]
    for u in (1, 0):
        qout[k, u] = qside.final(0, u)
    rows_k = pl.ds(k * 2, 2)
    out_core = rc(qout.at[k], qg_ref.at[rows_k], ms.at[4], mv.at[5 + k], core)
    out_here = pltpu.make_async_copy(qout.at[k], qg_ref.at[rows_k], osem.at[8])

    @pl.when(h == k)
    def _():
        out_here.start()

    @pl.when(h != k)
    def _():
        out_core.start()

    puts += [put_g(0, u) for u in (1, 0)]

    @pl.when(h == k)
    def _():
        out_here.wait()
        rc(qout.at[k], qg_ref.at[pl.ds((1 - k) * 2, 2)], ms.at[4], mv.at[6 - k], core).wait_recv()
        q1c.wait_send()

    @pl.when(h != k)
    def _():
        out_core.wait_send()
        moves = []
        for u in (1, 0):
            for kk in range(2):
                rc(qr_s.at[OUT], qo_r.at[kk, u], qs.at[1], ov.at[kk * 2 + u],
                   out_to).wait_recv()
                qout[kk, u] = decode(qo_r.at[kk, u], 512)
                c = pltpu.make_async_copy(
                    qout.at[kk, u], qg_ref.at[kk * 2 + u], osem.at[kk * 2 + u]
                )
                c.start()
                moves.append(c)
        for c in moves:
            c.wait()
        rc(q_ref, q_ref, ms.at[2], mv.at[2], core).wait_send()

    for c in puts:
        c.wait()
    pos_copy.wait_send()
    qside.sent(OUT + 2)
    gside.sent(OUT)


def hand_on(loss_in, qg_in, gg_in, loss_out, qg_out, gg_out, qv, gv, sem):
    ins, outs = [], []
    for i in range(4):
        a, b = pl.ds(i * 512, 512), pl.ds(i * 256, 256)
        for n, (src, mid, dst, r) in enumerate(((qg_in, qv, qg_out, a), (gg_in, gv, gg_out, b))):
            ins.append(pltpu.make_async_copy(src.at[r], mid.at[r], sem.at[0, i, n]))
            outs.append(pltpu.make_async_copy(mid.at[r], dst.at[r], sem.at[1, i, n]))
    for c in ins:
        c.start()
    loss_out[0, 0] = loss_in[0, 0]
    for c, d in zip(ins, outs):
        c.wait()
        d.start()
    for c in outs:
        c.wait()


def on_device(query_embed, gist_embed, positive):
    pos = positive.reshape(16, 128)
    vm, dma = pltpu.VMEM, pltpu.SemaphoreType.DMA
    scratch = [
        vm((4, 4, 1024, 128), BF16),
        vm((4, 2, 4, 512, 256), BF16),
        vm((16, 1024, 128), F32),
        vm((1024, 2048), BF16),
        vm((2048, 1024), BF16),
        vm((2, 16, 128), jnp.int32),
        vm((8, 128), F32),
        vm((8, 128), F32),
        vm((16, 8, 128), F32),
        vm((16, 8, 128), F32),
        vm((8, 2, 8, 128), F32),
        vm((2, 2, 2, 8, 128), F32),
        vm((8, 2, 2, 8, 128), F32),
        vm((16, 128), F32),
        vm((4, 8, 128), F32),
        vm((OUT + 2, 528, 128), I16),
        vm((NSLOT, 528, 128), I16),
        vm((OUT, 272, 256), I16),
        vm((NSLOT, 272, 256), I16),
        vm((2, 4, 528, 256), I16),
        vm((4, 4, 528, 256), I16),
        vm((4, 4, 512, 256), F32),
        vm((2, 2, 512, 128), F32),
        vm((2, 2, 528, 128), I16),
        vm((14, 8, 128), F32),
        dma((4,)), dma((NSLOT,)),
        dma((4,)), dma((NSLOT,)),
        dma((3,)), dma((3,)),
        dma((5,)), dma((7,)),
        dma, dma,
        dma, dma,
        dma((5,)), dma((5,)),
        dma((2,)), dma((4,)),
        dma((4,)),
        dma((4,)),
        dma((9,)),
    ]
    loss, qg, gg = pl.pallas_call(
        kernel,
        out_shape=[
            jax.ShapeDtypeStruct((8, 128), F32),
            jax.ShapeDtypeStruct((4, 512, 128), F32),
            jax.ShapeDtypeStruct((1024, 256), F32),
        ],
        in_specs=[
            pl.BlockSpec(memory_space=pl.ANY),
            pl.BlockSpec(memory_space=pl.ANY),
            pl.BlockSpec(memory_space=pltpu.VMEM),
        ],
        out_specs=[
            pl.BlockSpec(memory_space=pltpu.VMEM),
            pl.BlockSpec(memory_space=pl.ANY),
            pl.BlockSpec(memory_space=pl.ANY),
        ],
        scratch_shapes=scratch,
        compiler_params=pltpu.CompilerParams(
            collective_id=0, has_side_effects=True, vmem_limit_bytes=63 * 2**20
        ),
    )(query_embed, gist_embed, pos)
    loss, qg, gg = pl.pallas_call(
        hand_on,
        out_shape=[
            jax.ShapeDtypeStruct((1, 1), F32),
            jax.ShapeDtypeStruct((2048, 128), F32),
            jax.ShapeDtypeStruct((1024, 256), F32),
        ],
        in_specs=[
            pl.BlockSpec(memory_space=pltpu.VMEM),
            pl.BlockSpec(memory_space=pl.ANY),
            pl.BlockSpec(memory_space=pl.ANY),
        ],
        out_specs=[
            pl.BlockSpec(memory_space=pltpu.SMEM),
            pl.BlockSpec(memory_space=pl.ANY),
            pl.BlockSpec(memory_space=pl.ANY),
        ],
        scratch_shapes=[vm((2048, 128), F32), vm((1024, 256), F32), dma((2, 4, 2))],
    )(loss, qg.reshape(2048, 128), gg)
    return loss[0, 0], qg, gg


def solution(mesh):
    in_specs = (P("row", "col"), P("col", "row"), P("row"))
    out_specs = (P(), P("row", "col"), P("col", "row"))
    return jax.shard_map(
        on_device, mesh=mesh, in_specs=in_specs, out_specs=out_specs, check_vma=False
    )
```

```python
import functools
import math

import jax
import jax.numpy as jnp
from jax import lax
from jax.experimental import pallas as pl
from jax.experimental.pallas import tpu as pltpu
from jax.sharding import PartitionSpec as P

D = 2048
MESH = pl.DeviceIdType.MESH
LOG2E = 1.4426950408889634
LN2 = 0.6931471805599453
F32 = jnp.float32
BF16 = jnp.bfloat16
I16 = jnp.int16
TOP = 14.98

A, BP, BM, C, DD = 0, 4, 12, 20, 24
R1, R3P, R3M, R2, R3PH, R3MH, R4, NSLOT = 0, 4, 8, 12, 16, 20, 24, 28
OUT = R4


def where_am_i():
    row = lax.axis_index("row")
    col = lax.axis_index("col")
    return lax.div(col, 4), lax.div(row, 2), lax.rem(col, 4), lax.rem(row, 2)


def mod4(v):
    return lax.rem(v + 8, 4)


def encode(x):
    rows, cols = x.shape
    x3 = x.reshape(rows // 8, 8, cols)
    top = jnp.maximum(jnp.max(jnp.abs(x3), axis=0), 1e-30)
    e = jnp.ceil(jnp.log2(top) * 64.0)
    code = jnp.round(x3 * jnp.exp2(TOP - e * (1.0 / 64.0))[None]).reshape(rows, cols)
    return code.astype(jnp.int32).astype(I16), jnp.concatenate([e, e]).astype(jnp.int32).astype(I16)


def put(ref, v):
    rows = v.shape[0]
    code, e = encode(v)
    ref[pl.ds(0, rows), :] = code
    ref[pl.ds(rows, 16), :] = e


def decode(ref, rows):
    e = ref[pl.ds(rows, 16), :].astype(jnp.int32).astype(F32)[:8]
    x = ref[pl.ds(0, rows), :].astype(jnp.int32).astype(F32)
    x3 = x.reshape(rows // 8, 8, x.shape[1]) * jnp.exp2(e * (1.0 / 64.0) - TOP)[None]
    return x3.reshape(x.shape)


def kernel(
    q_ref, g_ref, pos_ref, loss_ref, qg_ref, gg_ref,
    qbuf, gbuf, s_buf, dl, dlt, posbuf,
    ml, sl, mc, sc, rowst, colst0, colst, cl_t, pacc,
    qr_s, qr_r, gr_s, gr_r, cx_s, cx_r, pg, qout, qo_r, lossbuf,
    qs, qv, gs, gv, es, ev, ms, mv, rs, rv, cs_, cv_, ls, lv, xs, xv, ov, lsem, osem,
):
    x, y, z, k = where_am_i()
    h = lax.div(x, 2)
    e = lax.rem(x, 2)
    xi = x + 1 - 2 * e
    xo = 3 - x
    xio = 3 - xi
    xj = [x, xo, xi, xio]

    def dev(xx, yy, zz, kk):
        return (yy * 2 + kk, xx * 4 + zz)

    core = dev(x, y, z, 1 - k)
    part_q = dev(xi, y, z, k)
    part_g = dev(xo, y, z, k)
    part_g2 = dev(xo, y, z, 1 - k)
    zpeer = {d: dev(x, y, mod4(z + d), k) for d in (1, 2, 3)}
    ypeer = {d: dev(x, mod4(y + d), z, k) for d in (1, 2, 3)}
    zipeer = {d: dev(xi, y, mod4(z + d), k) for d in (1, 2, 3)}
    yopeer = {d: dev(xo, mod4(y + d), z, k) for d in (1, 2, 3)}
    everyone = [core, part_q, part_g, part_g2]
    for group in (zpeer, ypeer, zipeer, yopeer):
        everyone += list(group.values())

    barrier = pltpu.get_barrier_semaphore()
    for other in everyone:
        pl.semaphore_signal(barrier, inc=1, device_id=other, device_id_type=MESH)

    def rc(src, dst, s, v, to):
        return pltpu.make_async_remote_copy(
            src_ref=src, dst_ref=dst, send_sem=s, recv_sem=v, device_id=to, device_id_type=MESH
        )

    gl = [
        pltpu.make_async_copy(g_ref.at[pl.ds(t * 512, 512)], gbuf.at[y, k, t], lsem.at[t])
        for t in range(2)
    ]
    for c in gl:
        c.start()
    here = pltpu.make_async_copy(q_ref.at[pl.ds(k * 1024, 1024)], qbuf.at[z, 0], lsem.at[2])
    posc = pltpu.make_async_copy(pos_ref, posbuf.at[k], lsem.at[3])
    posc.start()

    @pl.when(h == k)
    def _():
        here.start()

    pl.semaphore_wait(barrier, len(everyone))

    pos_copy = rc(pos_ref, posbuf.at[k], ms.at[0], mv.at[0], core)
    pos_copy.start()
    q1c = rc(q_ref.at[pl.ds((1 - k) * 1024, 1024)], qbuf.at[z, 0], ms.at[1], mv.at[1], core)
    q1o = [
        rc(q_ref.at[pl.ds(kk * 1024 + u * 512, 512)], qbuf.at[z, 1, pl.ds(u * 512, 512)],
           ms.at[2], mv.at[2 + u], dev(xo, y, z, kk))
        for u in range(2) for kk in range(2)
    ]

    @pl.when(h == k)
    def _():
        q1c.start()

    @pl.when(h != k)
    def _():
        for c in q1o:
            c.start()

    def qp(i, t, u):
        return qbuf.at[i, t, pl.ds(u * 512, 512)]

    def gp(i, t, u):
        return gbuf.at[i, k, t, pl.ds(u * 256, 256)]

    def ring(buf, r, sems, semv, plus, minus, partner):
        def msg(i, t, u, t2, idx, to):
            return rc(buf(i, t, u), buf(i, t2, u), sems.at[0], semv.at[idx], to)

        before, after, far = mod4(r - 1), mod4(r + 1), mod4(r + 2)
        m = {}
        for t in range(4):
            for u in range(2):
                n = t * 2 + u
                if t < 2:
                    m["a", t, u] = msg(r, t, u, t + 2, A + n, partner)
                    m["d", t, u] = msg(far, t, u, t + 2, DD + n, partner)
                    m["c", t, u] = msg(before if u == 0 else after, t, u, t, C + n,
                                       plus if u == 0 else minus)
                m["p", t, u] = msg(r, t, u, t, BP + n, plus)
                m["m", t, u] = msg(r, t, u, t, BM + n, minus)
        return m

    qm = ring(qp, z, qs, qv, zpeer[1], zpeer[3], part_q)
    gm = ring(gp, y, gs, gv, ypeer[1], ypeer[3], part_g)
    yb, ya, yf = mod4(y - 1), mod4(y + 1), mod4(y + 2)

    def start_core(i, t, u):
        rc(gp(i, t, u), gp(i, t, u), es.at[max(t - 1, 0)], ev.at[max(t - 1, 0)], core).start()

    def both(m, t, first):
        u = first
        m["p", t, u].start()
        m["m", t, 1 - u].start()

    def on(m, t):
        m["p", t, 0].wait_recv()
        m["c", t, 0].start()
        m["m", t, 1].wait_recv()
        m["c", t, 1].start()

    for c in gl:
        c.wait()
    both(gm, 0, 0)
    both(gm, 0, 1)
    for t in range(2):
        for u in range(2):
            gm["a", t, u].start()
    both(gm, 1, 0)

    @pl.when(h == k)
    def _():
        here.wait()

    @pl.when(h != k)
    def _():
        q1c.wait_recv()

    both(qm, 0, 0)
    both(qm, 0, 1)
    for u in range(2):
        qm["a", 0, u].start()
    for t in range(2):
        for u in range(2):
            start_core(y, t, u)
    on(gm, 0)
    on(qm, 0)
    both(gm, 1, 1)
    q1o[0].wait_recv()
    q1o[2].wait_recv()
    both(qm, 1, 0)
    qm["a", 1, 0].start()
    both(qm, 1, 1)
    qm["a", 1, 1].start()
    start_core(yb, 0, 0)
    start_core(ya, 0, 1)
    gm["p", 0, 1].wait_recv()
    start_core(yb, 0, 1)
    gm["m", 0, 0].wait_recv()
    start_core(ya, 0, 0)
    on(gm, 1)
    start_core(yb, 1, 0)
    start_core(ya, 1, 1)
    for u in range(2):
        gm["c", 0, u].wait_recv()
        gm["d", 0, u].start()
        start_core(yf, 0, u)
        qm["c", 0, u].wait_recv()
        qm["d", 0, u].start()
    on(qm, 1)
    for u in range(2):
        gm["a", 0, u].wait_recv()
        gm["p", 2, u].start()
        gm["m", 2, u].start()
        start_core(y, 2, u)
        qm["a", 0, u].wait_recv()
        qm["p", 2, u].start()
        qm["m", 2, u].start()
    gm["p", 1, 1].wait_recv()
    start_core(yb, 1, 1)
    gm["m", 1, 0].wait_recv()
    start_core(ya, 1, 0)
    for u in range(2):
        qm["a", 1, u].wait_recv()
        qm["p", 3, u].start()
        qm["m", 3, u].start()
        gm["a", 1, u].wait_recv()
        gm["p", 3, u].start()
        gm["m", 3, u].start()
        start_core(y, 3, u)
    for u in range(2):
        gm["c", 1, u].wait_recv()
        gm["d", 1, u].start()
        start_core(yf, 1, u)
        qm["c", 1, u].wait_recv()
        qm["d", 1, u].start()
    def all_core(n, mine):
        r = gbuf.at[:, mine, pl.ds(0, 2) if n == 0 else pl.ds(n + 1, 1)]
        return rc(r, r, es.at[n], ev.at[n], core)

    scale = LOG2E / math.sqrt(D)

    def logits(t, js, add):
        g = jnp.concatenate([gbuf[xj[j], m, t] for j in js for m in range(2)], axis=1)
        q = jnp.concatenate(
            [qbuf[2 * m + u, j] for j in js for m in range(2) for u in range(2)], axis=1
        )
        s = lax.dot_general(q, g, (((1,), (1,)), ((), ())), preferred_element_type=F32)
        s = s * scale
        for u in range(4):
            v = s[:, u * 128:(u + 1) * 128]
            s_buf[t * 4 + u] = s_buf[t * 4 + u] + v if add else v

    def queries_there(t):
        for u in range(2):
            if t >= 2 or u == 1:
                qm["p", t, u].wait_recv()
            if t >= 2 or u == 0:
                qm["m", t, u].wait_recv()
            if t >= 2:
                qm["d", t - 2, u].wait_recv()

    queries_there(0)
    queries_there(1)
    all_core(0, 1 - k).wait_recv()
    logits(0, (0, 1), False)
    logits(1, (0, 1), False)
    for t in range(2, 4):
        for u in range(2):
            gm["p", t, u].wait_recv()
            start_core(yb, t, u)
            gm["m", t, u].wait_recv()
            start_core(ya, t, u)
        if t == 2:
            for u in range(2):
                gm["d", 0, u].wait_recv()
                start_core(yf, 2, u)
            queries_there(2)
            all_core(1, 1 - k).wait_recv()
            logits(0, (2,), True)
            logits(1, (2,), True)
            logits(2, (0, 1, 2), False)
    for u in range(2):
        gm["d", 1, u].wait_recv()
        start_core(yf, 3, u)
    queries_there(3)
    posc.wait()
    pos_copy.wait_recv()

    def stats(t):
        for u in range(4):
            c = t * 4 + u
            v3 = s_buf[c].reshape(128, 8, 128)
            top = jnp.max(v3, axis=0)
            mc[c] = top
            sc[c] = jnp.sum(jnp.exp2(v3 - top[None]), axis=0)
        for b in range(2):
            for d in range(4):
                r, rb = pl.ds(b * 512 + d * 128, 128), pl.ds(d * 128, 128)
                v = [s_buf[t * 4 + u, r, :] for u in range(4)]
                top = jnp.maximum(jnp.maximum(v[0], v[1]), jnp.maximum(v[2], v[3]))
                if t > 0:
                    old = qout[0, b, rb, :]
                    top = jnp.maximum(old, top)
                e = [jnp.exp2(w - top) for w in v]
                total = (e[0] + e[1]) + (e[2] + e[3])
                if t > 0:
                    total = total + qout[1, b, rb, :] * jnp.exp2(old - top)
                qout[0, b, rb, :] = top
                qout[1, b, rb, :] = total

    for t in range(3):
        logits(t, (3,), True)
        if t > 0:
            stats(t - 1)
    all_core(2, 1 - k).wait_recv()
    logits(3, (0, 1, 2, 3), False)
    stats(2)
    stats(3)
    for c in range(16):
        peak = jnp.max(mc[c], axis=0, keepdims=True)
        one = jnp.sum(sc[c] * jnp.exp2(mc[c] - peak), axis=0, keepdims=True)
        colst0[0, c // 8, 0, pl.ds(c % 8, 1), :] = peak
        colst0[0, c // 8, 1, pl.ds(c % 8, 1), :] = one
    ccopy = rc(colst0.at[0], colst0.at[1], ms.at[3], mv.at[4], core)
    ccopy.start()

    for a in range(8):
        rb = pl.ds((a % 4) * 128, 128)
        tt = qout[0, a // 4, rb, :].T
        peak = jnp.max(tt, axis=0, keepdims=True)
        total = qout[1, a // 4, rb, :].T
        ml[pl.ds(a, 1), :] = peak
        sl[pl.ds(a, 1), :] = jnp.sum(total * jnp.exp2(tt - peak), axis=0, keepdims=True)

    me_row = e * 4 + z
    rowst[me_row, 0] = ml[...]
    rowst[me_row, 1] = sl[...]
    for to in list(zpeer.values()) + list(zipeer.values()) + [part_q]:
        rc(rowst.at[me_row], rowst.at[me_row], rs, rv, to).start()
    rall = rc(rowst.at[pl.ds(0, 7)], rowst.at[pl.ds(0, 7)], rs, rv, part_q)

    ccopy.wait()
    for i in range(2):
        m0, m1 = colst0[0, i, 0], colst0[1, i, 0]
        peak = jnp.maximum(m0, m1)
        colst[y, i, 0] = peak
        colst[y, i, 1] = colst0[0, i, 1] * jnp.exp2(m0 - peak) + colst0[1, i, 1] * jnp.exp2(
            m1 - peak
        )
    for to in ypeer.values():
        rc(colst.at[y], colst.at[y], cs_, cv_, to).start()
    for to in list(yopeer.values()) + [part_g]:
        rc(colst.at[y], colst.at[4 + y], cs_, cv_, to).start()
    kall = rc(colst.at[pl.ds(0, 7)], colst.at[pl.ds(0, 7)], cs_, cv_, part_g)

    for a in range(8):
        r = pl.ds((a % 4) * 128, 128)
        pos = posbuf[h, pl.ds(k * 8 + a, 1), :].astype(F32)
        qout[1, a // 4, r, :] = jnp.broadcast_to(pos, (128, 128)).T
    rall.wait()
    peak = rowst[0, 0]
    for n in range(1, 8):
        peak = jnp.maximum(peak, rowst[n, 0])
    tot = jnp.zeros_like(peak)
    for n in range(8):
        tot = tot + rowst[n, 1] * jnp.exp2(rowst[n, 0] - peak)
    row_lse = peak + jnp.log2(tot)
    ml[...] = row_lse

    for a in range(8):
        r = pl.ds((a % 4) * 128, 128)
        qout[0, a // 4, r, :] = jnp.broadcast_to(ml[pl.ds(a, 1), :], (128, 128)).T
    kall.wait()
    for i in range(2):
        peak = colst[0, i, 0]
        for n in range(4):
            peak = jnp.maximum(jnp.maximum(peak, colst[n, i, 0]), colst[4 + n, 1 - i, 0])
        tot = jnp.zeros_like(peak)
        for n in range(4):
            a0 = colst[n, i, 1] * jnp.exp2(colst[n, i, 0] - peak)
            a1 = colst[4 + n, 1 - i, 1] * jnp.exp2(colst[4 + n, 1 - i, 0] - peak)
            tot = tot + (a0 + a1)
        cl_t[pl.ds(i * 8, 8), :] = peak + jnp.log2(tot)

    lane = lax.broadcasted_iota(jnp.int32, (1, 128), 1)
    first = [(x * 4 + z) * 1024, (xo * 4 + z) * 1024]

    def dlogit(t):
        acc = jnp.zeros((8, 128), F32)
        for u in range(4):
            c = t * 4 + u
            cl = cl_t[pl.ds(c, 1), :]
            own = (lane + (first[c // 8] + (c % 8) * 128)).astype(F32)
            for a in range(8):
                r, rb = pl.ds(a * 128, 128), pl.ds((a % 4) * 128, 128)
                v = s_buf[c, r, :]
                hot = jnp.where(qout[1, a // 4, rb, :] == own, 2.0, 0.0)
                p = jnp.exp2(v - qout[0, a // 4, rb, :]) + jnp.exp2(v - cl) - hot
                acc = acc + jnp.sum((v * hot).reshape(16, 8, 128), axis=0)
                p = p.astype(BF16)
                dl[r, c * 128:(c + 1) * 128] = p
                dlt[c * 128:(c + 1) * 128, r] = p.T
        pacc[t] = acc

    dlogit(3)

    sub = lax.broadcasted_iota(jnp.int32, (8, 128), 0)
    lse_part = jnp.where(sub == me_row, row_lse, 0.0) + jnp.where(sub == y * 2 + k, cl_t[0:8, :], 0.0)
    loss_now = {}

    def loss_begin(n, v, slot, mine, count, to):
        lossbuf[slot + mine] = v
        for dst, other in to:
            rc(lossbuf.at[slot + mine], lossbuf.at[slot + dst], ls.at[n], lv.at[n], other).start()
        got = lossbuf.at[pl.ds(slot, count - 1)]
        loss_now[n] = rc(got, got, ls.at[n], lv.at[n], core)

    def loss_end(n, slot, count):
        loss_now[n].wait()
        v = [lossbuf[slot + i] for i in range(count)]
        while len(v) > 1:
            v = [v[i] + v[i + len(v) // 2] for i in range(len(v) // 2)]
        return v[0]

    to_a = [(me_row, to) for to in list(zpeer.values()) + list(zipeer.values()) + [part_q]]
    to_b = [(y, to) for to in ypeer.values()]
    to_b += [(4 + y, to) for to in list(yopeer.values()) + [part_g]]

    def grad_q(t):
        g = jnp.concatenate(
            [jnp.concatenate([gbuf[xj[t], m, i] for i in range(4)], axis=0) for m in range(2)],
            axis=1,
        )
        o = jnp.dot(dl[...], g, preferred_element_type=F32)
        for i in range(4):
            s_buf[i * 4 + t] = o[:, i * 128:(i + 1) * 128]

    def grad_g(t, rels, kk):
        cols = []
        for rel in rels:
            i = mod4(y + rel)
            j = jnp.where(i == x, 0, jnp.where(i == xo, 1, jnp.where(i == xi, 2, 3)))
            cols += [qbuf[2 * kk, j], qbuf[2 * kk + 1, j]]
        q = jnp.concatenate(cols, axis=1)
        return jnp.dot(dlt[t * 512:(t + 1) * 512, :], q, preferred_element_type=F32)

    for m, sem, ref in ((qm, qs, qbuf.at[:, :, pl.ds(0, 896)]),
                        (gm, gs, gbuf.at[:, k, :, pl.ds(0, 448)])):
        rc(ref, ref, sem.at[0], qv.at[0], core).wait_send()
    for n in range(3):
        all_core(n, k).wait_send()

    class Side:
        def __init__(self, get, rows, bufs, sems, plus, minus, partner):
            self.get, self.rows, self.bufs, self.sems = get, rows, bufs, sems
            self.plus, self.minus, self.partner = plus, minus, partner
            self.msgs = {}

        def send(self, *many):
            s, r = self.bufs
            cs, cv = self.sems
            copies = []
            for halves, slot, to in many:
                src, sem = slot, 1
                if slot >= R4:
                    src = slot - R4 + R1
                    self.msgs[src].wait_send()
                elif slot < R3P:
                    sem = 2 + (slot - R1) // 2
                here, there = pl.ds(src, len(halves)), pl.ds(slot, len(halves))
                c = rc(s.at[here], r.at[there], cs.at[sem], cv.at[slot], to)
                self.msgs[slot] = c
                copies.append(c)
                for n, v in enumerate(halves):
                    put(s.at[src + n], v)
            for c in copies:
                c.start()

        def sent(self, count):
            r = self.bufs[1].at[pl.ds(0, count)]
            rc(r, r, self.sems[0].at[1], self.sems[1].at[0], self.plus).wait_send()

        def arrive(self, slot):
            self.msgs[slot].wait_recv()

        def val(self, slot):
            return decode(self.bufs[1].at[slot], self.rows)

        def half(self, rel, t, u):
            return self.get(rel, t, pl.ds(u * self.rows, self.rows))

        def halves(self, rel, t):
            return [self.half(rel, t, u) for u in range(2)]

        def outer(self, t):
            n = (t - 2) * 2
            self.send(
                (self.halves(2, t), R1 + n, self.partner),
                (self.halves(1, t), R3P + n, self.plus),
                (self.halves(3, t), R3M + n, self.minus),
            )

        def inner(self, t):
            n = t * 2
            self.arrive(R1 + n)
            far = [self.half(2, t, u) + self.val(R1 + n + u) for u in range(2)]
            self.send(
                ([far[0]], R2 + n, self.plus),
                ([far[1]], R2 + n + 1, self.minus),
                ([self.half(1, t, 1)], R3PH + n + 1, self.plus),
                ([self.half(3, t, 0)], R3MH + n, self.minus),
            )

        def late(self, t):
            n = t * 2
            self.arrive(R2 + n)
            self.arrive(R2 + n + 1)
            self.send(
                ([self.half(1, t, 0) + self.val(R2 + n)], R3PH + n, self.plus),
                ([self.half(3, t, 1) + self.val(R2 + n + 1)], R3MH + n + 1, self.minus),
            )

        def across(self, t):
            n = (t - 2) * 2
            self.arrive(R3P + n)
            self.arrive(R3M + n)
            v = [
                self.half(0, t, u) + self.val(R3P + n + u) + self.val(R3M + n + u)
                for u in range(2)
            ]
            self.send((v, R4 + n, self.partner))

        def final(self, t, u):
            n = t * 2
            if ("4", t) not in self.msgs:
                self.arrive(R4 + n)
                self.msgs["4", t] = True
            self.arrive(R3PH + n + u)
            self.arrive(R3MH + n + u)
            return (
                (self.half(0, t, u) + self.val(R4 + n + u))
                + (self.val(R3PH + n + u) + self.val(R3MH + n + u))
            )

    qside = Side(
        lambda rel, t, r: s_buf[mod4(z + rel) * 4 + t, r, :], 512,
        (qr_s, qr_r), (qs, qv), zpeer[1], zpeer[3], part_q,
    )
    gside = Side(
        lambda rel, t, r: pg[rel, t, r, :], 256,
        (gr_s, gr_r), (gs, gv), ypeer[1], ypeer[3], part_g,
    )
    order = (2, 1, 3, 0)
    xmsg = {}

    def grad_g_other(t, beside=None, *args):
        if t < 2:
            xmsg[t + 2].wait_send()
        o = grad_g(t, order, 1 - k)
        if beside is not None:
            beside(*args)
        for n, rel in enumerate(order):
            put(cx_s.at[t % 2, rel], o[:, n * 256:(n + 1) * 256])
        xmsg[t] = rc(cx_s.at[t % 2], cx_r.at[t], xs.at[t % 2], xv.at[t], core)
        xmsg[t].start()

    def grad_g_own(t):
        o = grad_g(t, order, k)
        for n, rel in enumerate(order):
            pg[rel, t] = o[:, n * 256:(n + 1) * 256]

    def grad_g_sum(t):
        xmsg[t].wait_recv()
        for rel in order:
            pg[rel, t] += decode(cx_r.at[t, rel], 512)

    grad_g_other(3, dlogit, 0)
    grad_g_own(3)
    dlogit(1)
    dlogit(2)
    grad_q(3)
    qside.outer(3)
    grad_g_sum(3)
    gside.outer(3)
    hits = (pacc[0] + pacc[1]) + (pacc[2] + pacc[3])
    loss_begin(0, (lse_part - hits) * LN2, 0, 0, 2, [(1, core)])
    grad_g_other(2)
    grad_q(2)
    qside.outer(2)
    grad_g_own(2)
    grad_g_sum(2)
    gside.outer(2)
    loss_begin(1, loss_end(0, 0, 2), 2, me_row, 8, to_a)
    grad_g_other(1)
    grad_q(1)
    qside.inner(1)
    qside.across(3)
    grad_g_own(1)
    grad_g_sum(1)
    gside.inner(1)
    gside.across(3)
    grad_g_other(0)
    grad_q(0)
    qside.inner(0)
    qside.late(1)
    loss_begin(2, loss_end(1, 2, 8), 10, y, 8, to_b)
    grad_g_own(0)
    grad_g_sum(0)
    gside.inner(0)
    gside.late(1)
    qside.across(2)
    gside.across(2)
    qside.late(0)
    gside.late(0)
    loss = loss_end(2, 10, 8)
    loss = jnp.sum(jnp.sum(loss, axis=0, keepdims=True), axis=1, keepdims=True)
    loss_ref[...] = jnp.broadcast_to(loss * (1.0 / 32768.0), (8, 128))
    for t in (1, 0):
        xmsg[t].wait_send()

    out_to = dev(xo, y, z, h)
    out_sem = k * 2
    for u in (1, 0):
        put(qr_s.at[OUT + u], qside.final(1, u))
        rc(qr_s.at[OUT + u], qo_r.at[k, u], qs.at[1], ov.at[out_sem + u], out_to).start()

    def put_g(t, u):
        r = pl.ds(u * 256, 256)
        pg[0, t, r, :] = gside.final(t, u)
        n = t * 2 + u
        c = pltpu.make_async_copy(pg.at[0, t, r], gg_ref.at[pl.ds(n * 256, 256)], osem.at[4 + n])
        c.start()
        return c

    puts = [put_g(1, u) for u in (1, 0)]
    for u in (1, 0):
        qout[k, u] = qside.final(0, u)
    rows_k = pl.ds(k * 2, 2)
    out_core = rc(qout.at[k], qg_ref.at[rows_k], ms.at[4], mv.at[5 + k], core)
    out_here = pltpu.make_async_copy(qout.at[k], qg_ref.at[rows_k], osem.at[8])

    @pl.when(h == k)
    def _():
        out_here.start()

    @pl.when(h != k)
    def _():
        out_core.start()

    puts += [put_g(0, u) for u in (1, 0)]

    @pl.when(h == k)
    def _():
        out_here.wait()
        rc(qout.at[k], qg_ref.at[pl.ds((1 - k) * 2, 2)], ms.at[4], mv.at[6 - k], core).wait_recv()
        q1c.wait_send()

    @pl.when(h != k)
    def _():
        out_core.wait_send()
        moves = []
        for u in (1, 0):
            for kk in range(2):
                rc(qr_s.at[OUT], qo_r.at[kk, u], qs.at[1], ov.at[kk * 2 + u],
                   out_to).wait_recv()
                qout[kk, u] = decode(qo_r.at[kk, u], 512)
                c = pltpu.make_async_copy(
                    qout.at[kk, u], qg_ref.at[kk * 2 + u], osem.at[kk * 2 + u]
                )
                c.start()
                moves.append(c)
        for c in moves:
            c.wait()
        rc(q_ref, q_ref, ms.at[2], mv.at[2], core).wait_send()

    for c in puts:
        c.wait()
    pos_copy.wait_send()
    qside.sent(OUT + 2)
    gside.sent(OUT)


def hand_on(loss_in, qg_in, gg_in, loss_out, qg_out, gg_out, qv, gv, sem):
    ins, outs = [], []
    for i in range(4):
        a, b = pl.ds(i * 512, 512), pl.ds(i * 256, 256)
        for n, (src, mid, dst, r) in enumerate(((qg_in, qv, qg_out, a), (gg_in, gv, gg_out, b))):
            ins.append(pltpu.make_async_copy(src.at[r], mid.at[r], sem.at[0, i, n]))
            outs.append(pltpu.make_async_copy(mid.at[r], dst.at[r], sem.at[1, i, n]))
    for c in ins:
        c.start()
    loss_out[0, 0] = loss_in[0, 0]
    for c, d in zip(ins, outs):
        c.wait()
        d.start()
    for c in outs:
        c.wait()


def on_device(query_embed, gist_embed, positive):
    pos = positive.reshape(16, 128)
    vm, dma = pltpu.VMEM, pltpu.SemaphoreType.DMA
    scratch = [
        vm((4, 4, 1024, 128), BF16),
        vm((4, 2, 4, 512, 256), BF16),
        vm((16, 1024, 128), F32),
        vm((1024, 2048), BF16),
        vm((2048, 1024), BF16),
        vm((2, 16, 128), jnp.int32),
        vm((8, 128), F32),
        vm((8, 128), F32),
        vm((16, 8, 128), F32),
        vm((16, 8, 128), F32),
        vm((8, 2, 8, 128), F32),
        vm((2, 2, 2, 8, 128), F32),
        vm((8, 2, 2, 8, 128), F32),
        vm((16, 128), F32),
        vm((4, 8, 128), F32),
        vm((OUT + 2, 528, 128), I16),
        vm((NSLOT, 528, 128), I16),
        vm((OUT, 272, 256), I16),
        vm((NSLOT, 272, 256), I16),
        vm((2, 4, 528, 256), I16),
        vm((4, 4, 528, 256), I16),
        vm((4, 4, 512, 256), F32),
        vm((2, 2, 512, 128), F32),
        vm((2, 2, 528, 128), I16),
        vm((18, 8, 128), F32),
        dma((4,)), dma((NSLOT,)),
        dma((4,)), dma((NSLOT,)),
        dma((3,)), dma((3,)),
        dma((5,)), dma((7,)),
        dma, dma,
        dma, dma,
        dma((3,)), dma((3,)),
        dma((2,)), dma((4,)),
        dma((4,)),
        dma((4,)),
        dma((9,)),
    ]
    loss, qg, gg = pl.pallas_call(
        kernel,
        out_shape=[
            jax.ShapeDtypeStruct((8, 128), F32),
            jax.ShapeDtypeStruct((4, 512, 128), F32),
            jax.ShapeDtypeStruct((1024, 256), F32),
        ],
        in_specs=[
            pl.BlockSpec(memory_space=pl.ANY),
            pl.BlockSpec(memory_space=pl.ANY),
            pl.BlockSpec(memory_space=pltpu.VMEM),
        ],
        out_specs=[
            pl.BlockSpec(memory_space=pltpu.VMEM),
            pl.BlockSpec(memory_space=pl.ANY),
            pl.BlockSpec(memory_space=pl.ANY),
        ],
        scratch_shapes=scratch,
        compiler_params=pltpu.CompilerParams(
            collective_id=0, has_side_effects=True, vmem_limit_bytes=63 * 2**20
        ),
    )(query_embed, gist_embed, pos)
    loss, qg, gg = pl.pallas_call(
        hand_on,
        out_shape=[
            jax.ShapeDtypeStruct((1, 1), F32),
            jax.ShapeDtypeStruct((2048, 128), F32),
            jax.ShapeDtypeStruct((1024, 256), F32),
        ],
        in_specs=[
            pl.BlockSpec(memory_space=pltpu.VMEM),
            pl.BlockSpec(memory_space=pl.ANY),
            pl.BlockSpec(memory_space=pl.ANY),
        ],
        out_specs=[
            pl.BlockSpec(memory_space=pltpu.SMEM),
            pl.BlockSpec(memory_space=pl.ANY),
            pl.BlockSpec(memory_space=pl.ANY),
        ],
        scratch_shapes=[vm((2048, 128), F32), vm((1024, 256), F32), dma((2, 4, 2))],
    )(loss, qg.reshape(2048, 128), gg)
    return loss[0, 0], qg, gg


def solution(mesh):
    in_specs = (P("row", "col"), P("col", "row"), P("row"))
    out_specs = (P(), P("row", "col"), P("col", "row"))
    return jax.shard_map(
        on_device, mesh=mesh, in_specs=in_specs, out_specs=out_specs, check_vma=False
    )
```

```python
import functools
import math

import jax
import jax.numpy as jnp
from jax import lax
from jax.experimental import pallas as pl
from jax.experimental.pallas import tpu as pltpu
from jax.sharding import PartitionSpec as P

D = 2048
MESH = pl.DeviceIdType.MESH
LOG2E = 1.4426950408889634
LN2 = 0.6931471805599453
F32 = jnp.float32
BF16 = jnp.bfloat16
I16 = jnp.int16
TOP = 14.98

A, BP, BM, C, DD = 0, 4, 12, 20, 24
R1, R3P, R3M, R2, R3PH, R3MH, R4, NSLOT = 0, 4, 8, 12, 16, 20, 24, 28
OUT = R4


def where_am_i():
    row = lax.axis_index("row")
    col = lax.axis_index("col")
    return lax.div(col, 4), lax.div(row, 2), lax.rem(col, 4), lax.rem(row, 2)


def mod4(v):
    return lax.rem(v + 8, 4)


def encode(x):
    rows, cols = x.shape
    x3 = x.reshape(rows // 8, 8, cols)
    top = jnp.maximum(jnp.max(jnp.abs(x3), axis=0), 1e-30)
    e = jnp.ceil(jnp.log2(top) * 64.0)
    code = jnp.round(x3 * jnp.exp2(TOP - e * (1.0 / 64.0))[None]).reshape(rows, cols)
    return code.astype(jnp.int32).astype(I16), jnp.concatenate([e, e]).astype(jnp.int32).astype(I16)


def put(ref, v):
    rows = v.shape[0]
    code, e = encode(v)
    ref[pl.ds(0, rows), :] = code
    ref[pl.ds(rows, 16), :] = e


def decode(ref, rows):
    e = ref[pl.ds(rows, 16), :].astype(jnp.int32).astype(F32)[:8]
    x = ref[pl.ds(0, rows), :].astype(jnp.int32).astype(F32)
    x3 = x.reshape(rows // 8, 8, x.shape[1]) * jnp.exp2(e * (1.0 / 64.0) - TOP)[None]
    return x3.reshape(x.shape)


def kernel(
    q_ref, g_ref, pos_ref, loss_ref, qg_ref, gg_ref,
    qbuf, gbuf, s_buf, dl, dlt, posbuf,
    ml, sl, mc, sc, rowst, colst0, colst, cl_t, pacc,
    qr_s, qr_r, gr_s, gr_r, cx_s, cx_r, pg, qout, qo_r, lossbuf,
    qs, qv, gs, gv, es, ev, ms, mv, rs, rv, cs_, cv_, ls, lv, xs, xv, ov, lsem, osem,
):
    x, y, z, k = where_am_i()
    h = lax.div(x, 2)
    e = lax.rem(x, 2)
    xi = x + 1 - 2 * e
    xo = 3 - x
    xio = 3 - xi
    xj = [x, xo, xi, xio]

    def dev(xx, yy, zz, kk):
        return (yy * 2 + kk, xx * 4 + zz)

    core = dev(x, y, z, 1 - k)
    part_q = dev(xi, y, z, k)
    part_g = dev(xo, y, z, k)
    part_g2 = dev(xo, y, z, 1 - k)
    zpeer = {d: dev(x, y, mod4(z + d), k) for d in (1, 2, 3)}
    ypeer = {d: dev(x, mod4(y + d), z, k) for d in (1, 2, 3)}
    zipeer = {d: dev(xi, y, mod4(z + d), k) for d in (1, 2, 3)}
    yopeer = {d: dev(xo, mod4(y + d), z, k) for d in (1, 2, 3)}
    everyone = [core, part_q, part_g, part_g2]
    for group in (zpeer, ypeer, zipeer, yopeer):
        everyone += list(group.values())

    barrier = pltpu.get_barrier_semaphore()
    for other in everyone:
        pl.semaphore_signal(barrier, inc=1, device_id=other, device_id_type=MESH)

    def rc(src, dst, s, v, to):
        return pltpu.make_async_remote_copy(
            src_ref=src, dst_ref=dst, send_sem=s, recv_sem=v, device_id=to, device_id_type=MESH
        )

    gl = [
        pltpu.make_async_copy(g_ref.at[pl.ds(t * 512, 512)], gbuf.at[y, k, t], lsem.at[t])
        for t in range(2)
    ]
    for c in gl:
        c.start()
    here = pltpu.make_async_copy(q_ref.at[pl.ds(k * 1024, 1024)], qbuf.at[z, 0], lsem.at[2])
    posc = pltpu.make_async_copy(pos_ref, posbuf.at[k], lsem.at[3])
    posc.start()

    @pl.when(h == k)
    def _():
        here.start()

    pl.semaphore_wait(barrier, len(everyone))

    pos_copy = rc(pos_ref, posbuf.at[k], ms.at[0], mv.at[0], core)
    pos_copy.start()
    q1c = rc(q_ref.at[pl.ds((1 - k) * 1024, 1024)], qbuf.at[z, 0], ms.at[1], mv.at[1], core)
    q1o = [
        rc(q_ref.at[pl.ds(kk * 1024 + u * 512, 512)], qbuf.at[z, 1, pl.ds(u * 512, 512)],
           ms.at[2], mv.at[2 + u], dev(xo, y, z, kk))
        for u in range(2) for kk in range(2)
    ]

    @pl.when(h == k)
    def _():
        q1c.start()

    @pl.when(h != k)
    def _():
        for c in q1o:
            c.start()

    def qp(i, t, u):
        return qbuf.at[i, t, pl.ds(u * 512, 512)]

    def gp(i, t, u):
        return gbuf.at[i, k, t, pl.ds(u * 256, 256)]

    def ring(buf, r, sems, semv, plus, minus, partner):
        def msg(i, t, u, t2, idx, to):
            return rc(buf(i, t, u), buf(i, t2, u), sems.at[0], semv.at[idx], to)

        before, after, far = mod4(r - 1), mod4(r + 1), mod4(r + 2)
        m = {}
        for t in range(4):
            for u in range(2):
                n = t * 2 + u
                if t < 2:
                    m["a", t, u] = msg(r, t, u, t + 2, A + n, partner)
                    m["d", t, u] = msg(far, t, u, t + 2, DD + n, partner)
                    m["c", t, u] = msg(before if u == 0 else after, t, u, t, C + n,
                                       plus if u == 0 else minus)
                m["p", t, u] = msg(r, t, u, t, BP + n, plus)
                m["m", t, u] = msg(r, t, u, t, BM + n, minus)
        return m

    qm = ring(qp, z, qs, qv, zpeer[1], zpeer[3], part_q)
    gm = ring(gp, y, gs, gv, ypeer[1], ypeer[3], part_g)
    yb, ya, yf = mod4(y - 1), mod4(y + 1), mod4(y + 2)

    def start_core(i, t, u):
        rc(gp(i, t, u), gp(i, t, u), es.at[max(t - 1, 0)], ev.at[max(t - 1, 0)], core).start()

    def both(m, t, first):
        u = first
        m["p", t, u].start()
        m["m", t, 1 - u].start()

    def on(m, t):
        m["p", t, 0].wait_recv()
        m["c", t, 0].start()
        m["m", t, 1].wait_recv()
        m["c", t, 1].start()

    for c in gl:
        c.wait()
    both(gm, 0, 0)
    both(gm, 0, 1)
    for t in range(2):
        for u in range(2):
            gm["a", t, u].start()
    both(gm, 1, 0)

    @pl.when(h == k)
    def _():
        here.wait()

    @pl.when(h != k)
    def _():
        q1c.wait_recv()

    both(qm, 0, 0)
    both(qm, 0, 1)
    for u in range(2):
        qm["a", 0, u].start()
    for t in range(2):
        for u in range(2):
            start_core(y, t, u)
    on(gm, 0)
    on(qm, 0)
    both(gm, 1, 1)
    q1o[0].wait_recv()
    q1o[2].wait_recv()
    both(qm, 1, 0)
    qm["a", 1, 0].start()
    both(qm, 1, 1)
    qm["a", 1, 1].start()
    start_core(yb, 0, 0)
    start_core(ya, 0, 1)
    gm["p", 0, 1].wait_recv()
    start_core(yb, 0, 1)
    gm["m", 0, 0].wait_recv()
    start_core(ya, 0, 0)
    on(gm, 1)
    start_core(yb, 1, 0)
    start_core(ya, 1, 1)
    for u in range(2):
        gm["c", 0, u].wait_recv()
        gm["d", 0, u].start()
        start_core(yf, 0, u)
        qm["c", 0, u].wait_recv()
        qm["d", 0, u].start()
    on(qm, 1)
    for u in range(2):
        gm["a", 0, u].wait_recv()
        gm["p", 2, u].start()
        gm["m", 2, u].start()
        start_core(y, 2, u)
        qm["a", 0, u].wait_recv()
        qm["p", 2, u].start()
        qm["m", 2, u].start()
    gm["p", 1, 1].wait_recv()
    start_core(yb, 1, 1)
    gm["m", 1, 0].wait_recv()
    start_core(ya, 1, 0)
    for u in range(2):
        qm["a", 1, u].wait_recv()
        qm["p", 3, u].start()
        qm["m", 3, u].start()
        gm["a", 1, u].wait_recv()
        gm["p", 3, u].start()
        gm["m", 3, u].start()
        start_core(y, 3, u)
    for u in range(2):
        gm["c", 1, u].wait_recv()
        gm["d", 1, u].start()
        start_core(yf, 1, u)
        qm["c", 1, u].wait_recv()
        qm["d", 1, u].start()
    def all_core(n, mine):
        r = gbuf.at[:, mine, pl.ds(0, 2) if n == 0 else pl.ds(n + 1, 1)]
        return rc(r, r, es.at[n], ev.at[n], core)

    scale = LOG2E / math.sqrt(D)

    def logits(t, js, add):
        g = jnp.concatenate([gbuf[xj[j], m, t] for j in js for m in range(2)], axis=1)
        q = jnp.concatenate(
            [qbuf[2 * m + u, j] for j in js for m in range(2) for u in range(2)], axis=1
        )
        s = lax.dot_general(q, g, (((1,), (1,)), ((), ())), preferred_element_type=F32)
        s = s * scale
        for u in range(4):
            v = s[:, u * 128:(u + 1) * 128]
            s_buf[t * 4 + u] = s_buf[t * 4 + u] + v if add else v

    def queries_there(t):
        for u in range(2):
            if t >= 2 or u == 1:
                qm["p", t, u].wait_recv()
            if t >= 2 or u == 0:
                qm["m", t, u].wait_recv()
            if t >= 2:
                qm["d", t - 2, u].wait_recv()

    queries_there(0)
    queries_there(1)
    all_core(0, 1 - k).wait_recv()
    logits(0, (0, 1), False)
    logits(1, (0, 1), False)
    for t in range(2, 4):
        for u in range(2):
            gm["p", t, u].wait_recv()
            start_core(yb, t, u)
            gm["m", t, u].wait_recv()
            start_core(ya, t, u)
        if t == 2:
            for u in range(2):
                gm["d", 0, u].wait_recv()
                start_core(yf, 2, u)
            queries_there(2)
            all_core(1, 1 - k).wait_recv()
            logits(0, (2,), True)
            logits(1, (2,), True)
            logits(2, (0, 1, 2), False)
    for u in range(2):
        gm["d", 1, u].wait_recv()
        start_core(yf, 3, u)
    queries_there(3)
    posc.wait()
    pos_copy.wait_recv()

    def stats(t):
        for u in range(4):
            c = t * 4 + u
            v3 = s_buf[c].reshape(128, 8, 128)
            top = jnp.max(v3, axis=0)
            mc[c] = top
            sc[c] = jnp.sum(jnp.exp2(v3 - top[None]), axis=0)
        for b in range(2):
            for d in range(4):
                r, rb = pl.ds(b * 512 + d * 128, 128), pl.ds(d * 128, 128)
                v = [s_buf[t * 4 + u, r, :] for u in range(4)]
                top = jnp.maximum(jnp.maximum(v[0], v[1]), jnp.maximum(v[2], v[3]))
                if t > 0:
                    old = qout[0, b, rb, :]
                    top = jnp.maximum(old, top)
                e = [jnp.exp2(w - top) for w in v]
                total = (e[0] + e[1]) + (e[2] + e[3])
                if t > 0:
                    total = total + qout[1, b, rb, :] * jnp.exp2(old - top)
                qout[0, b, rb, :] = top
                qout[1, b, rb, :] = total

    for t in range(3):
        logits(t, (3,), True)
        if t > 0:
            stats(t - 1)
    all_core(2, 1 - k).wait_recv()
    logits(3, (0, 1, 2, 3), False)
    stats(2)
    stats(3)
    for c in range(16):
        peak = jnp.max(mc[c], axis=0, keepdims=True)
        one = jnp.sum(sc[c] * jnp.exp2(mc[c] - peak), axis=0, keepdims=True)
        colst0[0, c // 8, 0, pl.ds(c % 8, 1), :] = peak
        colst0[0, c // 8, 1, pl.ds(c % 8, 1), :] = one
    ccopy = rc(colst0.at[0], colst0.at[1], ms.at[3], mv.at[4], core)
    ccopy.start()

    for a in range(8):
        rb = pl.ds((a % 4) * 128, 128)
        tt = qout[0, a // 4, rb, :].T
        peak = jnp.max(tt, axis=0, keepdims=True)
        total = qout[1, a // 4, rb, :].T
        ml[pl.ds(a, 1), :] = peak
        sl[pl.ds(a, 1), :] = jnp.sum(total * jnp.exp2(tt - peak), axis=0, keepdims=True)

    me_row = e * 4 + z
    rowst[me_row, 0] = ml[...]
    rowst[me_row, 1] = sl[...]
    for to in list(zpeer.values()) + list(zipeer.values()) + [part_q]:
        rc(rowst.at[me_row], rowst.at[me_row], rs, rv, to).start()
    rall = rc(rowst.at[pl.ds(0, 7)], rowst.at[pl.ds(0, 7)], rs, rv, part_q)

    ccopy.wait()
    for i in range(2):
        m0, m1 = colst0[0, i, 0], colst0[1, i, 0]
        peak = jnp.maximum(m0, m1)
        colst[y, i, 0] = peak
        colst[y, i, 1] = colst0[0, i, 1] * jnp.exp2(m0 - peak) + colst0[1, i, 1] * jnp.exp2(
            m1 - peak
        )
    for to in ypeer.values():
        rc(colst.at[y], colst.at[y], cs_, cv_, to).start()
    for to in list(yopeer.values()) + [part_g]:
        rc(colst.at[y], colst.at[4 + y], cs_, cv_, to).start()
    kall = rc(colst.at[pl.ds(0, 7)], colst.at[pl.ds(0, 7)], cs_, cv_, part_g)

    for a in range(8):
        r = pl.ds((a % 4) * 128, 128)
        pos = posbuf[h, pl.ds(k * 8 + a, 1), :].astype(F32)
        qout[1, a // 4, r, :] = jnp.broadcast_to(pos, (128, 128)).T
    rall.wait()
    peak = rowst[0, 0]
    for n in range(1, 8):
        peak = jnp.maximum(peak, rowst[n, 0])
    tot = jnp.zeros_like(peak)
    for n in range(8):
        tot = tot + rowst[n, 1] * jnp.exp2(rowst[n, 0] - peak)
    row_lse = peak + jnp.log2(tot)
    ml[...] = row_lse

    for a in range(8):
        r = pl.ds((a % 4) * 128, 128)
        qout[0, a // 4, r, :] = jnp.broadcast_to(ml[pl.ds(a, 1), :], (128, 128)).T
    kall.wait()
    for i in range(2):
        peak = colst[0, i, 0]
        for n in range(4):
            peak = jnp.maximum(jnp.maximum(peak, colst[n, i, 0]), colst[4 + n, 1 - i, 0])
        tot = jnp.zeros_like(peak)
        for n in range(4):
            a0 = colst[n, i, 1] * jnp.exp2(colst[n, i, 0] - peak)
            a1 = colst[4 + n, 1 - i, 1] * jnp.exp2(colst[4 + n, 1 - i, 0] - peak)
            tot = tot + (a0 + a1)
        cl_t[pl.ds(i * 8, 8), :] = peak + jnp.log2(tot)

    lane = lax.broadcasted_iota(jnp.int32, (1, 128), 1)
    first = [(x * 4 + z) * 1024, (xo * 4 + z) * 1024]

    def dlogit(t):
        acc = jnp.zeros((8, 128), F32)
        for u in range(4):
            c = t * 4 + u
            cl = cl_t[pl.ds(c, 1), :]
            own = (lane + (first[c // 8] + (c % 8) * 128)).astype(F32)
            for a in range(8):
                r, rb = pl.ds(a * 128, 128), pl.ds((a % 4) * 128, 128)
                v = s_buf[c, r, :]
                hot = jnp.where(qout[1, a // 4, rb, :] == own, 2.0, 0.0)
                p = jnp.exp2(v - qout[0, a // 4, rb, :]) + jnp.exp2(v - cl) - hot
                acc = acc + jnp.sum((v * hot).reshape(16, 8, 128), axis=0)
                p = p.astype(BF16)
                dl[r, c * 128:(c + 1) * 128] = p
                dlt[c * 128:(c + 1) * 128, r] = p.T
        pacc[t] = acc

    dlogit(3)

    sub = lax.broadcasted_iota(jnp.int32, (8, 128), 0)
    lse_part = jnp.where(sub == me_row, row_lse, 0.0) + jnp.where(sub == y * 2 + k, cl_t[0:8, :], 0.0)
    loss_now = {}

    def loss_begin(n, v, slot, mine, count, to):
        lossbuf[slot + mine] = v
        for dst, other in to:
            rc(lossbuf.at[slot + mine], lossbuf.at[slot + dst], ls.at[n], lv.at[n], other).start()
        got = lossbuf.at[pl.ds(slot, count - 1)]
        loss_now[n] = rc(got, got, ls.at[n], lv.at[n], core)

    def loss_end(n, slot, count):
        loss_now[n].wait()
        v = [lossbuf[slot + i] for i in range(count)]
        while len(v) > 1:
            v = [v[i] + v[i + len(v) // 2] for i in range(len(v) // 2)]
        return v[0]

    to_a = [(me_row, to) for to in list(zpeer.values()) + list(zipeer.values()) + [part_q]]
    to_b = [(y, to) for to in ypeer.values()]
    to_b += [(4 + y, to) for to in list(yopeer.values()) + [part_g]]

    def grad_q(t):
        g = jnp.concatenate(
            [jnp.concatenate([gbuf[xj[t], m, i] for i in range(4)], axis=0) for m in range(2)],
            axis=1,
        )
        o = jnp.dot(dl[...], g, preferred_element_type=F32)
        for i in range(4):
            s_buf[i * 4 + t] = o[:, i * 128:(i + 1) * 128]

    def grad_g(t, rels, kk):
        cols = []
        for rel in rels:
            i = mod4(y + rel)
            j = jnp.where(i == x, 0, jnp.where(i == xo, 1, jnp.where(i == xi, 2, 3)))
            cols += [qbuf[2 * kk, j], qbuf[2 * kk + 1, j]]
        q = jnp.concatenate(cols, axis=1)
        return jnp.dot(dlt[t * 512:(t + 1) * 512, :], q, preferred_element_type=F32)

    for m, sem, ref in ((qm, qs, qbuf.at[:, :, pl.ds(0, 896)]),
                        (gm, gs, gbuf.at[:, k, :, pl.ds(0, 448)])):
        rc(ref, ref, sem.at[0], qv.at[0], core).wait_send()
    for n in range(3):
        all_core(n, k).wait_send()

    class Side:
        def __init__(self, get, rows, bufs, sems, plus, minus, partner):
            self.get, self.rows, self.bufs, self.sems = get, rows, bufs, sems
            self.plus, self.minus, self.partner = plus, minus, partner
            self.msgs = {}

        def send(self, *many):
            s, r = self.bufs
            cs, cv = self.sems
            copies = []
            for halves, slot, to in many:
                src, sem = slot, 1
                if slot >= R4:
                    src = slot - R4 + R1
                    self.msgs[src].wait_send()
                elif slot < R3P:
                    sem = 2 + (slot - R1) // 2
                here, there = pl.ds(src, len(halves)), pl.ds(slot, len(halves))
                c = rc(s.at[here], r.at[there], cs.at[sem], cv.at[slot], to)
                self.msgs[slot] = c
                copies.append(c)
                for n, v in enumerate(halves):
                    put(s.at[src + n], v)
            for c in copies:
                c.start()

        def sent(self, count):
            r = self.bufs[1].at[pl.ds(0, count)]
            rc(r, r, self.sems[0].at[1], self.sems[1].at[0], self.plus).wait_send()

        def arrive(self, slot):
            self.msgs[slot].wait_recv()

        def val(self, slot):
            return decode(self.bufs[1].at[slot], self.rows)

        def half(self, rel, t, u):
            return self.get(rel, t, pl.ds(u * self.rows, self.rows))

        def halves(self, rel, t):
            return [self.half(rel, t, u) for u in range(2)]

        def outer(self, t):
            n = (t - 2) * 2
            self.send(
                (self.halves(2, t), R1 + n, self.partner),
                (self.halves(1, t), R3P + n, self.plus),
                (self.halves(3, t), R3M + n, self.minus),
            )

        def inner(self, t):
            n = t * 2
            self.arrive(R1 + n)
            far = [self.half(2, t, u) + self.val(R1 + n + u) for u in range(2)]
            self.send(
                ([far[0]], R2 + n, self.plus),
                ([far[1]], R2 + n + 1, self.minus),
                ([self.half(1, t, 1)], R3PH + n + 1, self.plus),
                ([self.half(3, t, 0)], R3MH + n, self.minus),
            )

        def late(self, t):
            n = t * 2
            self.arrive(R2 + n)
            self.arrive(R2 + n + 1)
            self.send(
                ([self.half(1, t, 0) + self.val(R2 + n)], R3PH + n, self.plus),
                ([self.half(3, t, 1) + self.val(R2 + n + 1)], R3MH + n + 1, self.minus),
            )

        def across(self, t):
            n = (t - 2) * 2
            self.arrive(R3P + n)
            self.arrive(R3M + n)
            v = [
                self.half(0, t, u) + self.val(R3P + n + u) + self.val(R3M + n + u)
                for u in range(2)
            ]
            self.send((v, R4 + n, self.partner))

        def final(self, t, u):
            n = t * 2
            if ("4", t) not in self.msgs:
                self.arrive(R4 + n)
                self.msgs["4", t] = True
            self.arrive(R3PH + n + u)
            self.arrive(R3MH + n + u)
            return (
                (self.half(0, t, u) + self.val(R4 + n + u))
                + (self.val(R3PH + n + u) + self.val(R3MH + n + u))
            )

    qside = Side(
        lambda rel, t, r: s_buf[mod4(z + rel) * 4 + t, r, :], 512,
        (qr_s, qr_r), (qs, qv), zpeer[1], zpeer[3], part_q,
    )
    gside = Side(
        lambda rel, t, r: pg[rel, t, r, :], 256,
        (gr_s, gr_r), (gs, gv), ypeer[1], ypeer[3], part_g,
    )
    order = (2, 1, 3, 0)
    xmsg = {}

    def grad_g_other(t, beside=None, *args):
        if t < 2:
            xmsg[t + 2].wait_send()
        o = grad_g(t, order, 1 - k)
        if beside is not None:
            beside(*args)
        for n, rel in enumerate(order):
            put(cx_s.at[t % 2, rel], o[:, n * 256:(n + 1) * 256])
        xmsg[t] = rc(cx_s.at[t % 2], cx_r.at[t], xs.at[t % 2], xv.at[t], core)
        xmsg[t].start()

    def grad_g_own(t):
        o = grad_g(t, order, k)
        for n, rel in enumerate(order):
            pg[rel, t] = o[:, n * 256:(n + 1) * 256]

    def grad_g_sum(t):
        xmsg[t].wait_recv()
        for rel in order:
            pg[rel, t] += decode(cx_r.at[t, rel], 512)

    grad_g_other(3, dlogit, 0)
    grad_g_own(3)
    dlogit(1)
    dlogit(2)
    grad_q(3)
    qside.outer(3)
    grad_g_sum(3)
    gside.outer(3)
    hits = (pacc[0] + pacc[1]) + (pacc[2] + pacc[3])
    loss_begin(0, (lse_part - hits) * LN2, 0, 0, 2, [(1, core)])
    grad_g_other(2)
    grad_q(2)
    qside.outer(2)
    grad_g_own(2)
    grad_g_sum(2)
    gside.outer(2)
    loss_begin(1, loss_end(0, 0, 2), 2, me_row, 8, to_a)
    grad_g_other(1)
    grad_q(1)
    qside.inner(1)
    qside.across(3)
    grad_g_own(1)
    grad_g_sum(1)
    gside.inner(1)
    gside.across(3)
    grad_g_other(0)
    grad_q(0)
    qside.inner(0)
    qside.late(1)
    loss_begin(2, loss_end(1, 2, 8), 10, y, 8, to_b)
    grad_g_own(0)
    qside.across(2)
    grad_g_sum(0)
    gside.inner(0)
    gside.late(1)
    gside.across(2)
    qside.late(0)
    gside.late(0)
    for t in (1, 0):
        xmsg[t].wait_send()

    out_to = dev(xo, y, z, h)
    out_sem = k * 2
    for u in (1, 0):
        put(qr_s.at[OUT + u], qside.final(1, u))
        rc(qr_s.at[OUT + u], qo_r.at[k, u], qs.at[1], ov.at[out_sem + u], out_to).start()

    def put_g(t, u):
        r = pl.ds(u * 256, 256)
        pg[0, t, r, :] = gside.final(t, u)
        n = t * 2 + u
        c = pltpu.make_async_copy(pg.at[0, t, r], gg_ref.at[pl.ds(n * 256, 256)], osem.at[4 + n])
        c.start()
        return c

    puts = [put_g(1, u) for u in (1, 0)]
    for u in (1, 0):
        qout[k, u] = qside.final(0, u)
    rows_k = pl.ds(k * 2, 2)
    out_core = rc(qout.at[k], qg_ref.at[rows_k], ms.at[4], mv.at[5 + k], core)
    out_here = pltpu.make_async_copy(qout.at[k], qg_ref.at[rows_k], osem.at[8])

    @pl.when(h == k)
    def _():
        out_here.start()

    @pl.when(h != k)
    def _():
        out_core.start()

    puts += [put_g(0, u) for u in (1, 0)]
    loss = loss_end(2, 10, 8)
    loss = jnp.sum(jnp.sum(loss, axis=0, keepdims=True), axis=1, keepdims=True)
    loss_ref[...] = jnp.broadcast_to(loss * (1.0 / 32768.0), (8, 128))

    @pl.when(h == k)
    def _():
        out_here.wait()
        rc(qout.at[k], qg_ref.at[pl.ds((1 - k) * 2, 2)], ms.at[4], mv.at[6 - k], core).wait_recv()
        q1c.wait_send()

    @pl.when(h != k)
    def _():
        out_core.wait_send()
        moves = []
        for u in (1, 0):
            for kk in range(2):
                rc(qr_s.at[OUT], qo_r.at[kk, u], qs.at[1], ov.at[kk * 2 + u],
                   out_to).wait_recv()
                qout[kk, u] = decode(qo_r.at[kk, u], 512)
                c = pltpu.make_async_copy(
                    qout.at[kk, u], qg_ref.at[kk * 2 + u], osem.at[kk * 2 + u]
                )
                c.start()
                moves.append(c)
        for c in moves:
            c.wait()
        rc(q_ref, q_ref, ms.at[2], mv.at[2], core).wait_send()

    for c in puts:
        c.wait()
    pos_copy.wait_send()
    qside.sent(OUT + 2)
    gside.sent(OUT)


def hand_on(loss_in, qg_in, gg_in, loss_out, qg_out, gg_out, qv, gv, sem):
    ins, outs = [], []
    for i in range(4):
        a, b = pl.ds(i * 512, 512), pl.ds(i * 256, 256)
        for n, (src, mid, dst, r) in enumerate(((qg_in, qv, qg_out, a), (gg_in, gv, gg_out, b))):
            ins.append(pltpu.make_async_copy(src.at[r], mid.at[r], sem.at[0, i, n]))
            outs.append(pltpu.make_async_copy(mid.at[r], dst.at[r], sem.at[1, i, n]))
    for c in ins:
        c.start()
    loss_out[0, 0] = loss_in[0, 0]
    for c, d in zip(ins, outs):
        c.wait()
        d.start()
    for c in outs:
        c.wait()


def on_device(query_embed, gist_embed, positive):
    pos = positive.reshape(16, 128)
    vm, dma = pltpu.VMEM, pltpu.SemaphoreType.DMA
    scratch = [
        vm((4, 4, 1024, 128), BF16),
        vm((4, 2, 4, 512, 256), BF16),
        vm((16, 1024, 128), F32),
        vm((1024, 2048), BF16),
        vm((2048, 1024), BF16),
        vm((2, 16, 128), jnp.int32),
        vm((8, 128), F32),
        vm((8, 128), F32),
        vm((16, 8, 128), F32),
        vm((16, 8, 128), F32),
        vm((8, 2, 8, 128), F32),
        vm((2, 2, 2, 8, 128), F32),
        vm((8, 2, 2, 8, 128), F32),
        vm((16, 128), F32),
        vm((4, 8, 128), F32),
        vm((OUT + 2, 528, 128), I16),
        vm((NSLOT, 528, 128), I16),
        vm((OUT, 272, 256), I16),
        vm((NSLOT, 272, 256), I16),
        vm((2, 4, 528, 256), I16),
        vm((4, 4, 528, 256), I16),
        vm((4, 4, 512, 256), F32),
        vm((2, 2, 512, 128), F32),
        vm((2, 2, 528, 128), I16),
        vm((18, 8, 128), F32),
        dma((4,)), dma((NSLOT,)),
        dma((4,)), dma((NSLOT,)),
        dma((3,)), dma((3,)),
        dma((5,)), dma((7,)),
        dma, dma,
        dma, dma,
        dma((3,)), dma((3,)),
        dma((2,)), dma((4,)),
        dma((4,)),
        dma((4,)),
        dma((9,)),
    ]
    loss, qg, gg = pl.pallas_call(
        kernel,
        out_shape=[
            jax.ShapeDtypeStruct((8, 128), F32),
            jax.ShapeDtypeStruct((4, 512, 128), F32),
            jax.ShapeDtypeStruct((1024, 256), F32),
        ],
        in_specs=[
            pl.BlockSpec(memory_space=pl.ANY),
            pl.BlockSpec(memory_space=pl.ANY),
            pl.BlockSpec(memory_space=pltpu.VMEM),
        ],
        out_specs=[
            pl.BlockSpec(memory_space=pltpu.VMEM),
            pl.BlockSpec(memory_space=pl.ANY),
            pl.BlockSpec(memory_space=pl.ANY),
        ],
        scratch_shapes=scratch,
        compiler_params=pltpu.CompilerParams(
            collective_id=0, has_side_effects=True, vmem_limit_bytes=63 * 2**20
        ),
    )(query_embed, gist_embed, pos)
    loss, qg, gg = pl.pallas_call(
        hand_on,
        out_shape=[
            jax.ShapeDtypeStruct((1, 1), F32),
            jax.ShapeDtypeStruct((2048, 128), F32),
            jax.ShapeDtypeStruct((1024, 256), F32),
        ],
        in_specs=[
            pl.BlockSpec(memory_space=pltpu.VMEM),
            pl.BlockSpec(memory_space=pl.ANY),
            pl.BlockSpec(memory_space=pl.ANY),
        ],
        out_specs=[
            pl.BlockSpec(memory_space=pltpu.SMEM),
            pl.BlockSpec(memory_space=pl.ANY),
            pl.BlockSpec(memory_space=pl.ANY),
        ],
        scratch_shapes=[vm((2048, 128), F32), vm((1024, 256), F32), dma((2, 4, 2))],
    )(loss, qg.reshape(2048, 128), gg)
    return loss[0, 0], qg, gg


def solution(mesh):
    in_specs = (P("row", "col"), P("col", "row"), P("row"))
    out_specs = (P(), P("row", "col"), P("col", "row"))
    return jax.shard_map(
        on_device, mesh=mesh, in_specs=in_specs, out_specs=out_specs, check_vma=False
    )
```
